512 devices in a mesh: panel: 2 (over core), lon: 16 (over y_lo, x), lat: 16 (over y_hi, z).
Axes of the slice: x: 4, y: 8 (y_hi: 2, y_lo: 4; y = y_hi * 4 + y_lo), z: 8, core: 2. Of those that a mesh axis runs over, the one named last changes fastest.
Arguments:
- motion_and_stress: float32 [4, 2, 32, 256, 2048], P(None, 'panel', None, 'lat', 'lon'), may hold values from -6 to 6
- warmth: float32 [2, 32, 256, 2048], P('panel', None, 'lat', 'lon'), may hold values from 0 to 1
- substance_label: int32 [2, 32, 256, 2048], P('panel', None, 'lat', 'lon'), may hold values from 0 to 7
- substance_stiffness_exponent: float32 [8], replicated, may hold values from -2.3 to 2.3
- receiver_indices: int32 [2, 16, 16, 512], P('panel', 'lat', 'lon'), may hold values from 0 to 2047, as said below
- donor_indices: int32 [2, 16, 16, 4, 512], P('panel', 'lat', 'lon'), may hold values from 0 to 2047
- blend_factors: float32 [2, 16, 16, 4, 512], P('panel', 'lat', 'lon'), may hold values from 0.1 to 0.4
Outputs:
- flow_out: float32 [4, 2, 32, 256, 2048], P(None, 'panel', None, 'lat', 'lon')
- temperature_out: float32 [2, 32, 256, 2048], P('panel', None, 'lat', 'lon')
The draws below stay inside these ranges and needn't reach their ends.
Inputs may be any that keep to these rules, and one draw needn't show every extreme that they name: `receiver_indices`: the 512 targets of one tile are distinct cells of that tile.
All inputs are finite; a program needn't handle non-finite values.
Results may differ from the reference program's by a relative error of at most 0.00011.
Values sent between devices are 32-bit elements; how exact they have to be, the bound alone decides.
No kernel may reach another device: no remote copies, remote signals or barrier semaphores. Data moves between devices by JAX's collectives and lax.ppermute only.
A program may use at most 128 MiB of HBM per device.

```python
import jax
import jax.numpy as jnp

DEPTH_LAYERS = 32
CLAT = 16
CLON = 128
OVL = 512
SWEEPS = 2
PHASES = 8
NORTHSOUTH_SITES = 256
EASTWEST_SITES = 2048
N_LON = 16
N_LAT = 16


def draw_receiver_indices(key, part):
    key = jax.random.fold_in(key, 11)
    tile_keys = jax.random.split(key, 2 * N_LAT * N_LON)
    picked = jax.vmap(lambda tile_key: jax.random.permutation(tile_key, CLAT * CLON)[:OVL])(tile_keys)
    return picked.reshape(2, N_LAT, N_LON, OVL).astype(jnp.int32)


def with_ends(array, stream_key, least, largest):
    shape = array.shape
    place = [jax.random.randint(jax.random.fold_in(stream_key, axis), (), 0, shape[axis]) for axis in range(len(shape))]
    array = array.at[tuple(place)].set(least)
    longest = shape.index(max(shape))
    place[longest] = (place[longest] + 1) % shape[longest]
    return array.at[tuple(place)].set(largest)


def steps_of(rng, shape, cuts, low, top_value):
    gain, own = 1.0, jax.random.fold_in(rng, 6)
    for position, blocks in cuts:
        heights = jnp.exp(jax.random.uniform(jax.random.fold_in(own, position), (blocks,), jnp.float32, low / len(cuts), top_value / len(cuts)))
        gain = gain * jnp.repeat(heights, shape[position] // blocks).reshape([-1 if axis == position else 1 for axis in range(len(shape))])
    return gain


def gaussian(rng, dims, width, limit, cuts=(), kind=jnp.bfloat16):
    loudness = steps_of(rng, dims, cuts, -0.22, 0.18) if cuts else 1.0
    entries = jax.random.normal(rng, dims, jnp.float32) * width * loudness
    return jnp.minimum(jnp.maximum(entries, -limit), limit).astype(kind)


def setup_inputs(seed: int = 0) -> dict:
    keys = jax.random.split(jax.random.key(seed), 8)
    return {
        "motion_and_stress": gaussian(keys[0], (4, 2, DEPTH_LAYERS, NORTHSOUTH_SITES, EASTWEST_SITES), 1.0, 6.0, ((1, 2), (3, 16), (4, 16)), jnp.float32),
        "warmth": jnp.clip(1.0 * jax.random.uniform(keys[1], (2, DEPTH_LAYERS, NORTHSOUTH_SITES, EASTWEST_SITES), jnp.float32) ** steps_of(keys[1], (2, DEPTH_LAYERS, NORTHSOUTH_SITES, EASTWEST_SITES), ((0, 2), (2, 16), (3, 16)), -0.2, 0.2), 0.0, 1.0),
        "substance_label": with_ends(jax.random.randint(keys[2], (2, DEPTH_LAYERS, NORTHSOUTH_SITES, EASTWEST_SITES), 0, PHASES), jax.random.fold_in(keys[2], 1), 0, PHASES - 1).astype(jnp.int32),
        "substance_stiffness_exponent": jnp.clip(jax.random.uniform(keys[3], (PHASES,), jnp.float32, -2.3, 2.3), -2.3, 2.3),
        "receiver_indices": draw_receiver_indices(jax.random.fold_in(keys[7], 71), 0),
        "donor_indices": with_ends(jax.random.randint(keys[5], (2, N_LAT, N_LON, 4, OVL), 0, CLAT * CLON), jax.random.fold_in(keys[5], 1), 0, (CLAT * CLON) - 1).astype(jnp.int32),
        "blend_factors": jnp.clip(0.1 + 0.3 * jax.random.uniform(keys[6], (2, N_LAT, N_LON, 4, OVL), jnp.float32) ** steps_of(keys[6], (2, N_LAT, N_LON, 4, OVL), ((0, 2), (1, 16), (2, 16)), -0.2, 0.2), 0.1, 0.4),
    }


OMEGA = 0.6
BETA = 0.5
KAPPA = 1.0
TIME_STEP = 0.05
LIFT_FACTOR = 2.0
DIFFUSIVITY = 2.3


def neighbour(padded, direction, offset):
    window = [slice(1, -1), slice(1, -1), slice(1, -1)]
    extent = padded.shape[padded.ndim - 3 + direction]
    window[direction] = slice(1 + offset, extent - 1 + offset)
    leading = tuple(slice(None) for _ in range(padded.ndim - 3))
    return padded[leading + tuple(window)]


def stiffness_array(substance_label, warmth, reference_chart):
    logarithm_value = jnp.zeros(substance_label.shape, jnp.float32)
    for entry in range(reference_chart.shape[0]):
        logarithm_value = logarithm_value + jnp.where(substance_label == entry, reference_chart[entry], 0.0)
    return jnp.exp(logarithm_value + DIFFUSIVITY * (0.5 - warmth))


def relax_flow(padded_flow, padded_eta, lifting_push):
    centre_eta = neighbour(padded_eta, 0, 0)
    centre = neighbour(padded_flow, 0, 0)
    diagonal = jnp.zeros_like(centre_eta)
    face_flux = jnp.zeros_like(centre[:3])
    for direction in range(3):
        for offset in (-1, 1):
            face_eta = 0.5 * (centre_eta + neighbour(padded_eta, direction, offset))
            diagonal = diagonal + face_eta
            face_flux = face_flux + face_eta * (neighbour(padded_flow[:3], direction, offset) - centre[:3])
    pressure_grad = jnp.stack([0.5 * (neighbour(padded_flow[3], component, 1) - neighbour(padded_flow[3], component, -1)) for component in range(3)])
    divergence = jnp.zeros_like(centre_eta)
    for component in range(3):
        divergence = divergence + 0.5 * (neighbour(padded_flow[component], component, 1) - neighbour(padded_flow[component], component, -1))
    zero_part = jnp.zeros_like(lifting_push)
    push = jnp.stack([lifting_push, zero_part, zero_part])
    velocity = centre[:3] + OMEGA * (push + face_flux - pressure_grad) / diagonal
    pressure = centre[3] - BETA * centre_eta * divergence
    return jnp.concatenate([velocity, pressure[None]], 0)


def carry_warmth(padded_temp, velocity):
    centre = neighbour(padded_temp, 0, 0)
    change = jnp.zeros_like(centre)
    for direction in range(3):
        upper = neighbour(padded_temp, direction, 1)
        lower = neighbour(padded_temp, direction, -1)
        speed = velocity[direction]
        change = change - jnp.maximum(speed, 0.0) * (centre - lower) - jnp.minimum(speed, 0.0) * (upper - centre) + KAPPA * (upper + lower - 2.0 * centre)
    return centre + TIME_STEP * change


def blend_between(tile_flat, donor_sequence, blend_factor_sequence):
    total = blend_factor_sequence[0] * jnp.take(tile_flat, donor_sequence[0], axis=2)
    for entry in range(1, 4):
        total = total + blend_factor_sequence[entry] * jnp.take(tile_flat, donor_sequence[entry], axis=2)
    return total


def insert_numbers(tile_flat, receiver_sequence, incoming):
    return tile_flat.at[:, :, receiver_sequence].set(incoming)


def border_all_arrays(field):
    return jnp.pad(field, [(0, 0)] * (field.ndim - 3) + [(1, 1)] * 3)


def to_tiles(fields):
    number = fields.shape[0]
    tile_view = fields.reshape(number, 2, DEPTH_LAYERS, N_LAT, CLAT, N_LON, CLON)
    tile_view = tile_view.transpose(1, 3, 5, 0, 2, 4, 6)
    return tile_view.reshape(2, N_LAT, N_LON, number, DEPTH_LAYERS, CLAT * CLON)


def from_tiles(tile_view):
    number = tile_view.shape[3]
    fields = tile_view.reshape(2, N_LAT, N_LON, number, DEPTH_LAYERS, CLAT, CLON)
    fields = fields.transpose(3, 0, 4, 1, 5, 2, 6)
    return fields.reshape(number, 2, DEPTH_LAYERS, N_LAT * CLAT, N_LON * CLON)


def reference(motion_and_stress, warmth, substance_label, substance_stiffness_exponent, receiver_indices, donor_indices, blend_factors):
    local_stiffness = stiffness_array(substance_label, warmth, substance_stiffness_exponent)
    lifting_push = LIFT_FACTOR * (warmth - 0.5)
    padded_eta = border_all_arrays(local_stiffness)
    relaxed_motion = motion_and_stress
    for sweep_index in range(SWEEPS):
        relaxed_motion = relax_flow(border_all_arrays(relaxed_motion), padded_eta, lifting_push)
    warmed_result = carry_warmth(border_all_arrays(warmth), relaxed_motion[:3])
    fields = jnp.concatenate([relaxed_motion, warmed_result[None]], 0)
    tile_view = to_tiles(fields)
    per_tile = jax.vmap(jax.vmap(jax.vmap(blend_between)))
    numbers = per_tile(tile_view, donor_indices, blend_factors)
    incoming = numbers[::-1, :, ::-1]
    tile_view = jax.vmap(jax.vmap(jax.vmap(insert_numbers)))(tile_view, receiver_indices, incoming)
    fields = from_tiles(tile_view)
    return fields[:4], fields[4]
```

```python
import jax
import jax.numpy as jnp
from jax import lax
from jax.experimental import pallas as pl
from jax.experimental.pallas import tpu as pltpu
from jax.sharding import PartitionSpec as P

OMEGA = 0.6
BETA = 0.5
TIME_STEP = 0.05
DIFFUSIVITY = 2.3

F32 = jnp.float32
BF16 = jnp.bfloat16
ANY = pl.BlockSpec(memory_space=pl.ANY)
VMEM = pl.BlockSpec(memory_space=pltpu.VMEM)
SMEM = pl.BlockSpec(memory_space=pltpu.SMEM)

LAT, DEP, LON = 16, 32, 128


def iota(dim, shape=(DEP, LON)):
    return lax.broadcasted_iota(jnp.int32, shape, dim)


def roll(x, shift, axis):
    return pltpu.roll(x, shift, axis)


def depth_pair(x):
    row = iota(0, x.shape)
    lower = jnp.where(row == 0, 0.0, roll(x, 1, 0))
    upper = jnp.where(row == x.shape[0] - 1, 0.0, roll(x, x.shape[0] - 1, 0))
    return lower, upper


def lon_pair(x, edge, r):
    lane = iota(1, x.shape)
    halo = roll(edge, 122 - 4 * r, 1)
    lower = jnp.where(lane == 0, halo, roll(x, 1, 1))
    upper = jnp.where(lane == LON - 1, halo, roll(x, LON - 1, 1))
    return lower, upper


def swap_middle(c):
    pos = iota(1, c.shape) & 3
    return jnp.where(pos == 1, roll(c, LON - 1, 1), roll(c, 1, 1))


def relax(centre, pairs, faces, scale, eta, warmth):
    out = []
    for c in range(3):
        total = 0.0
        for e in range(3):
            for s in range(2):
                total = total + faces[e][s] * pairs[c][e][s]
        total = total - (pairs[3][c][1] - pairs[3][c][0])
        if c == 0:
            total = total + 4.0 * (warmth - 0.5)
        out.append((1.0 - OMEGA) * centre[c] + total * scale)
    div = 0.0
    for c in range(3):
        div = div + (pairs[c][c][1] - pairs[c][c][0])
    out.append(centre[3] - (0.5 * BETA) * eta * div)
    return out


def edges_kernel(motion, warmth, label, chart, eta_out, cols_out, up_out, down_out, m, t, lab, sems):
    copies = []
    for r in range(LAT):
        copies.append(pltpu.make_async_copy(warmth.at[0, :, r, :], t.at[r], sems.at[0, r]))
        copies.append(pltpu.make_async_copy(label.at[0, :, r, :], lab.at[r], sems.at[1, r]))
    for r in range(LAT):
        copies.append(pltpu.make_async_copy(motion.at[:, 0, :, r, :], m.at[:, r], sems.at[2, r]))
    for c in copies:
        c.start()
    for c in copies:
        c.wait()

    def stiffness(r, _):
        kind = lab[r]
        exponent = jnp.full(kind.shape, chart[0], F32)
        for entry in range(1, 8):
            exponent = jnp.where(kind == entry, chart[entry], exponent)
        eta_out[r] = jnp.exp(exponent + DIFFUSIVITY * (0.5 - t[r]))
        return 0

    lax.fori_loop(0, LAT, stiffness, 0)

    group = iota(1) >> 2

    def pack(r, acc):
        fields = (m[0, r], m[1, r], m[2, r], m[3, r], eta_out[r], t[r])
        new = []
        for q in range(3):
            first = roll(fields[2 * q], 4 * r + 2, 1)
            second = roll(fields[2 * q + 1], 4 * r + 66, 1)
            new.append(jnp.where(group == r, first, jnp.where(group == r + 16, second, acc[q])))
        return tuple(new)

    zero = jnp.zeros((DEP, LON), F32)
    packed = lax.fori_loop(0, LAT, pack, (zero, zero, zero))
    for q in range(3):
        cols_out[q] = packed[q]
    for out, outer, inner in ((up_out, 14, 15), (down_out, 1, 0)):
        for f in range(4):
            out[f] = m[f, outer]
            out[5 + f] = m[f, inner]
        out[4] = eta_out[outer]
        out[9] = eta_out[inner]
        out[10] = t[inner]
        out[11] = zero


def corners_kernel(left, right, up, down, up_out, down_out, cu, cd, sems):
    lane = iota(1)
    pos = lane & 3
    group = (lane >> 2) & 15
    pairs = [jnp.where(pos < 2, left[q], right[q]) for q in range(3)]
    cu[...] = jnp.where(group == 15, pairs[0], jnp.where(group == 14, roll(pairs[1], 124, 1), roll(pairs[2], 120, 1)))
    cd[...] = jnp.where(group == 0, pairs[0], jnp.where(group == 1, roll(pairs[1], 4, 1), roll(pairs[2], 8, 1)))
    a = pltpu.make_async_copy(cu, up_out.at[11], sems.at[0])
    b = pltpu.make_async_copy(cd, down_out.at[11], sems.at[1])
    a.start()
    b.start()
    a.wait()
    b.wait()


def weights_kernel(donors, factors, hi, lo):
    def body(i, _):
        cell = iota(0, (32, 512)) + i * 32
        w = jnp.zeros((32, 512), F32)
        for j in range(4):
            w = w + jnp.where(cell == donors[j : j + 1, :], factors[j : j + 1, :], 0.0)
        top = w.astype(BF16)
        at = pl.ds(pl.multiple_of(i * 32, 32), 32)
        hi[at, :] = top
        lo[at, :] = (w - top.astype(F32)).astype(BF16)
        return 0

    lax.fori_loop(0, LAT * LON // 32, body, 0)


def table_kernel(receivers, table):
    def body(i, _):
        cell = iota(0, (32, 512)) + i * 32
        table[pl.ds(pl.multiple_of(i * 32, 32), 32), :] = jnp.where(cell == receivers[...], 1.0, 0.0).astype(BF16)
        return 0

    lax.fori_loop(0, LAT * LON // 32, body, 0)


def flow_kernel(motion, warmth, eta, cols, left, right, south, north, whi, wlo, fields_out, values_out, f, s1, faces, edge, lhs, sems):
    copies = []
    for r in range(LAT):
        copies.append(pltpu.make_async_copy(motion.at[:, 0, :, r, :], f.at[0:4, r + 2], sems.at[0, r]))
        copies.append(pltpu.make_async_copy(warmth.at[0, :, r, :], f.at[5, r + 2], sems.at[1, r]))
    copies.append(pltpu.make_async_copy(eta, f.at[4, 2:18], sems.at[2, 0]))
    copies.append(pltpu.make_async_copy(south.at[0:5], f.at[0:5, 0], sems.at[2, 1]))
    copies.append(pltpu.make_async_copy(south.at[5:11], f.at[:, 1], sems.at[2, 2]))
    copies.append(pltpu.make_async_copy(north.at[0:5], f.at[0:5, 19], sems.at[2, 3]))
    copies.append(pltpu.make_async_copy(north.at[5:11], f.at[:, 18], sems.at[2, 4]))
    corner_s, corner_n = edge.at[10], edge.at[11]
    copies.append(pltpu.make_async_copy(south.at[11], corner_s, sems.at[2, 5]))
    copies.append(pltpu.make_async_copy(north.at[11], corner_n, sems.at[2, 6]))
    for c in copies:
        c.start()
    for c in copies:
        c.wait()

    lane = iota(1)
    pos = lane & 3
    group = lane >> 2
    middle = pos == 1

    halo, own = [], []
    for k in range(6):
        q, h = k // 2, k % 2
        both = jnp.where(pos < 2, left[q], right[q])
        c = roll(both, 4 + 64 * h, 1)
        low = roll(corner_s[...], (128 - (64 * h + 60 - 4 * q)) % 128, 1)
        high = roll(corner_n[...], (68 - 64 * h - 4 * q) % 128, 1)
        c = jnp.where(group == 0, low, jnp.where(group == 17, high, c))
        halo.append(c)
        own.append(roll(cols[q], 4 + 64 * h, 1))
        edge[k] = swap_middle(c)

    def column_pairs(k):
        c, o = halo[k], own[k]
        lower = jnp.where(middle, roll(c, 1, 1), roll(o, 1, 1))
        upper = jnp.where(middle, roll(o, LON - 1, 1), roll(c, LON - 1, 1))
        return depth_pair(c), (roll(c, 4, 1), roll(c, LON - 4, 1)), (lower, upper)

    eta_pairs = column_pairs(4)
    col_faces = [[halo[4] + n for n in pair] for pair in eta_pairs]
    diagonal = 0.0
    for pair in col_faces:
        diagonal = diagonal + pair[0] + pair[1]
    inside = halo[4] > 0.0
    scale = OMEGA / jnp.where(inside, diagonal, 1.0)
    new = relax(halo[:4], [column_pairs(k) for k in range(4)], col_faces, scale, halo[4], halo[5])
    for k in range(4):
        edge[6 + k] = swap_middle(jnp.where(inside, new[k], 0.0))

    def first(i, _):
        r = i - 1
        eta_c = f[4, i + 1]
        eta_pairs = (depth_pair(eta_c), (f[4, i], f[4, i + 2]), lon_pair(eta_c, edge[4], r))
        both = [[eta_c + n for n in pair] for pair in eta_pairs]
        diagonal = both[0][0] + both[0][1] + both[1][0] + both[1][1] + both[2][0] + both[2][1]
        scale = OMEGA / diagonal
        faces[0, i] = both[0][0]
        faces[1, i] = both[0][1]
        faces[2, i] = both[2][0]
        faces[3, i] = both[2][1]
        faces[4, i] = scale
        centre = [f[k, i + 1] for k in range(4)]
        pairs = [(depth_pair(centre[k]), (f[k, i], f[k, i + 2]), lon_pair(centre[k], edge[k], r)) for k in range(4)]
        new = relax(centre, pairs, both, scale, eta_c, f[5, i + 1])
        for k in range(4):
            s1[k, i] = new[k]
        return 0

    lax.fori_loop(0, LAT + 2, first, 0)
    for i in (0, LAT + 1):
        here = f[4, i + 1] > 0.0
        for k in range(4):
            s1[k, i] = jnp.where(here, s1[k, i], 0.0)

    def second(r, _):
        i = r + 1
        eta_c = f[4, r + 2]
        both = [
            (faces[0, i], faces[1, i]),
            (eta_c + f[4, r + 1], eta_c + f[4, r + 3]),
            (faces[2, i], faces[3, i]),
        ]
        centre = [s1[k, i] for k in range(4)]
        pairs = [(depth_pair(centre[k]), (s1[k, i - 1], s1[k, i + 1]), lon_pair(centre[k], edge[6 + k], r)) for k in range(4)]
        t = f[5, r + 2]
        new = relax(centre, pairs, both, faces[4, i], eta_c, t)
        change = 0.0
        for e, (lower, upper) in enumerate((depth_pair(t), (f[5, r + 1], f[5, r + 3]), lon_pair(t, edge[5], r))):
            change = (
                change
                - jnp.maximum(new[e], 0.0) * (t - lower)
                - jnp.minimum(new[e], 0.0) * (upper - t)
                + (upper + lower - 2.0 * t)
            )
        new.append(t + TIME_STEP * change)
        at = pl.ds(pl.multiple_of(r * LON, LON), LON)
        for k in range(5):
            fields_out[k, r] = new[k]
            top = new[k].astype(BF16)
            lhs[k * DEP : (k + 1) * DEP, at] = top
            lhs[(5 + k) * DEP : (6 + k) * DEP, at] = (new[k] - top.astype(F32)).astype(BF16)
        return 0

    lax.fori_loop(0, LAT, second, 0)
    n = 5 * DEP
    wide = jnp.dot(lhs[...], whi[...], preferred_element_type=F32)
    values_out[...] = wide[:n] + wide[n:] + jnp.dot(lhs[:n], wlo[...], preferred_element_type=F32)


def place_kernel(fields, values, table, flow_out, warmth_out, lhs, out, sems):
    n = 5 * DEP
    v = values[...]
    top = v.astype(BF16)
    lhs[0:n] = top
    lhs[n : 2 * n] = (v - top.astype(F32)).astype(BF16)
    lhs[2 * n : 2 * n + 16] = jnp.ones((16, 512), BF16)
    copies = []
    for g in range(LAT // 2):
        rows = table[g * 256 : (g + 1) * 256, :]
        placed = lax.dot_general(lhs[...], rows, (((1,), (1,)), ((), ())), preferred_element_type=F32)
        struck = placed[2 * n : 2 * n + 1] > 0.5
        merged = placed[:n] + placed[n : 2 * n]
        for h in range(2):
            r = 2 * g + h
            at = slice(h * LON, (h + 1) * LON)
            for k in range(5):
                out[k, r] = jnp.where(struck[:, at], merged[k * DEP : (k + 1) * DEP, at], fields[k, r])
            copies.append(pltpu.make_async_copy(out.at[0:4, r], flow_out.at[:, 0, :, r, :], sems.at[0, r]))
            copies.append(pltpu.make_async_copy(out.at[4, r], warmth_out.at[0, :, r, :], sems.at[1, r]))
            copies[-2].start()
            copies[-1].start()
    for c in copies:
        c.wait()


def shape(*dims, dtype=F32):
    return jax.ShapeDtypeStruct(dims, dtype)


def call(kernel, outs, ins, scratch=(), out_specs=None, flops=0, size=0, aliases=None, limit=None):
    return pl.pallas_call(
        kernel,
        out_shape=outs,
        in_specs=ins,
        out_specs=out_specs or [VMEM] * len(outs),
        scratch_shapes=list(scratch),
        input_output_aliases=aliases or {},
        cost_estimate=pl.CostEstimate(flops=flops, bytes_accessed=size, transcendentals=0),
        compiler_params=pltpu.CompilerParams(vmem_limit_bytes=limit or (32 << 20)),
    )


def shards(motion, warmth, label, chart, receivers, donors, factors):
    lon, lat = lax.axis_size("lon"), lax.axis_size("lat")
    receivers = receivers.reshape(1, 512)
    donors = donors.reshape(4, 512)
    factors = factors.reshape(4, 512)

    slab = (LAT, DEP, LON)
    eta, cols, up, down = call(
        edges_kernel,
        [shape(*slab), shape(3, DEP, LON), shape(12, DEP, LON), shape(12, DEP, LON)],
        [ANY, ANY, ANY, SMEM],
        [pltpu.VMEM((4,) + slab, F32), pltpu.VMEM(slab, F32), pltpu.VMEM(slab, jnp.int32), pltpu.SemaphoreType.DMA((3, LAT))],
        size=2 << 20,
    )(motion, warmth, label, chart)

    ahead = lambda n: [(i, i + 1) for i in range(n - 1)]
    back = lambda n: [(i + 1, i) for i in range(n - 1)]
    left = lax.ppermute(cols, "lon", ahead(lon))
    right = lax.ppermute(cols, "lon", back(lon))
    up, down = call(
        corners_kernel,
        [shape(12, DEP, LON), shape(12, DEP, LON)],
        [VMEM, VMEM, ANY, ANY],
        [pltpu.VMEM((DEP, LON), F32), pltpu.VMEM((DEP, LON), F32), pltpu.SemaphoreType.DMA((2,))],
        out_specs=[ANY, ANY],
        aliases={2: 0, 3: 1},
        size=1 << 16,
    )(left, right, up, down)
    south = lax.ppermute(up, "lat", ahead(lat))
    north = lax.ppermute(down, "lat", back(lat))

    whi, wlo = call(
        weights_kernel,
        [shape(LAT * LON, 512, dtype=BF16), shape(LAT * LON, 512, dtype=BF16)],
        [VMEM, VMEM],
        size=4 << 20,
        flops=20 << 20,
    )(donors, factors)

    fields, values = call(
        flow_kernel,
        [shape(5, *slab), shape(5 * DEP, 512)],
        [ANY, ANY, ANY, VMEM, VMEM, VMEM, ANY, ANY, VMEM, VMEM],
        [
            pltpu.VMEM((6, LAT + 4, DEP, LON), F32),
            pltpu.VMEM((4, LAT + 2, DEP, LON), F32),
            pltpu.VMEM((5, LAT + 2, DEP, LON), F32),
            pltpu.VMEM((12, DEP, LON), F32),
            pltpu.VMEM((10 * DEP, LAT * LON), BF16),
            pltpu.SemaphoreType.DMA((3, LAT)),
        ],
        size=8 << 20,
        flops=1 << 30,
    )(motion, warmth, eta, cols, left, right, south, north, whi, wlo)

    mirror = [(p * lon + b, (1 - p) * lon + lon - 1 - b) for p in range(2) for b in range(lon)]
    incoming = lax.ppermute(values, ("panel", "lon"), mirror)

    (table,) = call(table_kernel, [shape(LAT * LON, 512, dtype=BF16)], [VMEM], size=2 << 20, flops=4 << 20)(receivers)

    flow, warm = call(
        place_kernel,
        [shape(4, 1, DEP, LAT, LON), shape(1, DEP, LAT, LON)],
        [VMEM, VMEM, VMEM],
        [pltpu.VMEM((10 * DEP + 16, 512), BF16), pltpu.VMEM((5,) + slab, F32), pltpu.SemaphoreType.DMA((2, LAT))],
        out_specs=[ANY, ANY],
        size=8 << 20,
        flops=1 << 30,
    )(fields, incoming, table)
    return flow, warm


def solution(mesh):
    field = P("panel", None, "lat", "lon")
    tile = ("panel", "lat", "lon")
    in_specs = (
        P(None, "panel", None, "lat", "lon"),
        field,
        field,
        P(),
        P(*tile, None),
        P(*tile, None, None),
        P(*tile, None, None),
    )
    out_specs = (P(None, "panel", None, "lat", "lon"), field)
    return jax.shard_map(shards, mesh=mesh, in_specs=in_specs, out_specs=out_specs, check_vma=False)
```

```python
import jax
import jax.numpy as jnp
from jax import lax
from jax.experimental import pallas as pl
from jax.experimental.pallas import tpu as pltpu
from jax.sharding import PartitionSpec as P

OMEGA = 0.6
BETA = 0.5
TIME_STEP = 0.05
DIFFUSIVITY = 2.3

F32 = jnp.float32
BF16 = jnp.bfloat16
ANY = pl.BlockSpec(memory_space=pl.ANY)
VMEM = pl.BlockSpec(memory_space=pltpu.VMEM)
HBM = pl.BlockSpec(memory_space=pltpu.HBM)

LAT, DEP, LON = 16, 32, 128


def iota(dim, shape=(DEP, LON)):
    return lax.broadcasted_iota(jnp.int32, shape, dim)


def roll(x, shift, axis):
    return pltpu.roll(x, shift, axis)


def depth_pair(x):
    row = iota(0, x.shape)
    lower = jnp.where(row == 0, 0.0, roll(x, 1, 0))
    upper = jnp.where(row == x.shape[0] - 1, 0.0, roll(x, x.shape[0] - 1, 0))
    return lower, upper


def lon_pair(x, edge, r):
    lane = iota(1, x.shape)
    halo = roll(edge, 122 - 4 * r, 1)
    lower = jnp.where(lane == 0, halo, roll(x, 1, 1))
    upper = jnp.where(lane == LON - 1, halo, roll(x, LON - 1, 1))
    return lower, upper


def swap_middle(c):
    pos = iota(1, c.shape) & 3
    return jnp.where(pos == 1, roll(c, LON - 1, 1), roll(c, 1, 1))


def relax(centre, pairs, faces, scale, eta, warmth):
    out = []
    for c in range(3):
        total = 0.0
        for e in range(3):
            for s in range(2):
                total = total + faces[e][s] * pairs[c][e][s]
        total = total - (pairs[3][c][1] - pairs[3][c][0])
        if c == 0:
            total = total + 4.0 * (warmth - 0.5)
        out.append((1.0 - OMEGA) * centre[c] + total * scale)
    div = 0.0
    for c in range(3):
        div = div + (pairs[c][c][1] - pairs[c][c][0])
    out.append(centre[3] - (0.5 * BETA) * eta * div)
    return out


def stage_kernel(
    motion, warmth, label, chart, receivers, donors, factors,
    f, cols_out, up_out, down_out, receivers_out, donors_out, factors_out,
    lab, table, sems,
):
    small = [
        pltpu.make_async_copy(chart, table, sems.at[3, 0]),
        pltpu.make_async_copy(receivers, receivers_out, sems.at[3, 1]),
        pltpu.make_async_copy(donors, donors_out, sems.at[3, 2]),
        pltpu.make_async_copy(factors, factors_out, sems.at[3, 3]),
    ]
    scalars, flow = [], []
    for r in range(LAT):
        scalars.append(pltpu.make_async_copy(warmth.at[0, :, r, :], f.at[5, r], sems.at[0, r]))
        scalars.append(pltpu.make_async_copy(label.at[0, :, r, :], lab.at[r], sems.at[1, r]))
        flow.append(pltpu.make_async_copy(motion.at[:, 0, :, r, :], f.at[0:4, r], sems.at[2, r]))
    for c in small[:1] + scalars + flow + small[1:]:
        c.start()
    for c in small[:1] + scalars:
        c.wait()

    def stiffness(r, _):
        kind = lab[r]
        exponent = jnp.full(kind.shape, table[0], F32)
        for entry in range(1, 8):
            exponent = jnp.where(kind == entry, table[entry], exponent)
        f[4, r] = jnp.exp(exponent + DIFFUSIVITY * (0.5 - f[5, r]))
        return 0

    lax.fori_loop(0, LAT, stiffness, 0, unroll=4)
    for c in flow:
        c.wait()

    group = iota(1) >> 2

    def pack(r, acc):
        new = []
        for q in range(3):
            first = roll(f[2 * q, r], 4 * r + 2, 1)
            second = roll(f[2 * q + 1, r], 4 * r + 66, 1)
            new.append(jnp.where(group == r, first, jnp.where(group == r + 16, second, acc[q])))
        return tuple(new)

    zero = jnp.zeros((DEP, LON), F32)
    packed = lax.fori_loop(0, LAT, pack, (zero, zero, zero), unroll=4)
    for q in range(3):
        cols_out[q] = packed[q]
    for out, outer, inner in ((up_out, 14, 15), (down_out, 1, 0)):
        for k in range(5):
            out[k] = f[k, outer]
        for k in range(6):
            out[5 + k] = f[k, inner]
        out[11] = zero
    for c in small[1:]:
        c.wait()


def corners_kernel(left, right, up, down, _, up_out, down_out, cu, cd, sems):
    lane = iota(1)
    pos = lane & 3
    group = (lane >> 2) & 15
    pairs = [jnp.where(pos < 2, left[q], right[q]) for q in range(3)]
    cu[...] = jnp.where(group == 15, pairs[0], jnp.where(group == 14, roll(pairs[1], 124, 1), roll(pairs[2], 120, 1)))
    cd[...] = jnp.where(group == 0, pairs[0], jnp.where(group == 1, roll(pairs[1], 4, 1), roll(pairs[2], 8, 1)))
    a = pltpu.make_async_copy(cu, up_out.at[11], sems.at[0])
    b = pltpu.make_async_copy(cd, down_out.at[11], sems.at[1])
    a.start()
    b.start()
    a.wait()
    b.wait()


def weights_kernel(donors, factors, hi, lo):
    def body(i, _):
        cell = iota(0, (32, 512)) + i * 32
        w = jnp.zeros((32, 512), F32)
        for j in range(4):
            w = w + jnp.where(cell == donors[j : j + 1, :], factors[j : j + 1, :], 0.0)
        top = w.astype(BF16)
        at = pl.ds(pl.multiple_of(i * 32, 32), 32)
        hi[at, :] = top
        lo[at, :] = (w - top.astype(F32)).astype(BF16)
        return 0

    lax.fori_loop(0, LAT * LON // 32, body, 0)


def table_kernel(receivers, table, struck):
    columns = []
    for b in range(4):
        row = receivers[:, b * 128 : (b + 1) * 128].astype(F32)
        columns.append(jnp.broadcast_to(row, (128, 128)).T.astype(jnp.int32))

    def body(i, _):
        cell = iota(1, (128, LON)) + i * LON
        at = pl.ds(pl.multiple_of(i * LON, LON), LON)
        total = jnp.zeros((1, LON), F32)
        for b in range(4):
            hit = jnp.where(cell == columns[b], 1.0, 0.0)
            table[b * 128 : (b + 1) * 128, at] = hit.astype(BF16)
            total = total + jnp.sum(hit, axis=0, keepdims=True)
        struck[:, at] = jnp.broadcast_to(total, (8, LON))
        return 0

    lax.fori_loop(0, LAT, body, 0)


def edge_columns(cols, left, right, corners):
    lane = iota(1)
    pos, group = lane & 3, lane >> 2
    halo, own = [], []
    for k in range(6):
        q, h = k // 2, k % 2
        c = roll(jnp.where(pos < 2, left[q], right[q]), 4 + 64 * h, 1)
        low = high = 0.0
        if corners is not None:
            low = roll(corners[0], (68 + 64 * h + 4 * q) % 128, 1)
            high = roll(corners[1], (68 + 64 * h - 4 * q) % 128, 1)
        halo.append(jnp.where(group == 0, low, jnp.where(group == 17, high, c)))
        own.append(roll(cols[q], 4 + 64 * h, 1))
    return halo, own


def relax_columns(halo, own):
    middle = (iota(1) & 3) == 1

    def pairs_of(k):
        c, o = halo[k], own[k]
        lower = jnp.where(middle, roll(c, 1, 1), roll(o, 1, 1))
        upper = jnp.where(middle, roll(o, LON - 1, 1), roll(c, LON - 1, 1))
        return depth_pair(c), (roll(c, 4, 1), roll(c, LON - 4, 1)), (lower, upper)

    faces, scale = faces_of(halo[4], pairs_of(4))
    inside = halo[4] > 0.0
    new = relax(halo[:4], [pairs_of(k) for k in range(4)], faces, scale, halo[4], halo[5])
    return [jnp.where(inside, v, 0.0) for v in new]


def faces_of(eta, pairs):
    faces = [[eta + n for n in pair] for pair in pairs]
    diagonal = faces[0][0] + faces[0][1] + faces[1][0] + faces[1][1] + faces[2][0] + faces[2][1]
    return faces, OMEGA / jnp.where(diagonal > 0.0, diagonal, 1.0)


def advance(t, pairs, speed):
    change = 0.0
    for e, (lower, upper) in enumerate(pairs):
        change = (
            change
            - jnp.maximum(speed[e], 0.0) * (t - lower)
            - jnp.minimum(speed[e], 0.0) * (upper - t)
            + (upper + lower - 2.0 * t)
        )
    return t + TIME_STEP * change


def blend(lhs, hi, lo):
    n = 5 * DEP
    wide = jnp.dot(lhs, hi, preferred_element_type=F32)
    return wide[:n] + wide[n:] + jnp.dot(lhs[:n], lo, preferred_element_type=F32)


def put_split(lhs, k, at, value):
    top = value.astype(BF16)
    lhs[k * DEP : (k + 1) * DEP, at] = top
    lhs[(5 + k) * DEP : (6 + k) * DEP, at] = (value - top.astype(F32)).astype(BF16)


def inner_kernel(f, cols, left, right, whi, wlo, mid_out, values_out, s1_out, faces_out, s1, faces, edge, lhs):
    halo, own = edge_columns(cols, left, right, None)
    for k in range(6):
        edge[k] = swap_middle(halo[k])
    for k, v in enumerate(relax_columns(halo, own)):
        edge[6 + k] = swap_middle(v)

    def first(r, _):
        eta = f[4, r]
        both, scale = faces_of(eta, (depth_pair(eta), (f[4, r - 1], f[4, r + 1]), lon_pair(eta, edge[4], r)))
        for j, v in enumerate((both[0][0], both[0][1], both[2][0], both[2][1], scale)):
            faces[j, r] = v
        centre = [f[k, r] for k in range(4)]
        pairs = [(depth_pair(centre[k]), (f[k, r - 1], f[k, r + 1]), lon_pair(centre[k], edge[k], r)) for k in range(4)]
        for k, v in enumerate(relax(centre, pairs, both, scale, eta, f[5, r])):
            s1[k, r] = v
        return 0

    lax.fori_loop(1, LAT - 1, first, 0)

    def second(r, _):
        eta = f[4, r]
        both = ((faces[0, r], faces[1, r]), (eta + f[4, r - 1], eta + f[4, r + 1]), (faces[2, r], faces[3, r]))
        centre = [s1[k, r] for k in range(4)]
        pairs = [(depth_pair(centre[k]), (s1[k, r - 1], s1[k, r + 1]), lon_pair(centre[k], edge[6 + k], r)) for k in range(4)]
        t = f[5, r]
        new = relax(centre, pairs, both, faces[4, r], eta, t)
        new.append(advance(t, (depth_pair(t), (f[5, r - 1], f[5, r + 1]), lon_pair(t, edge[5], r)), new))
        at = pl.ds(pl.multiple_of((r - 2) * LON, LON), LON)
        for k in range(5):
            mid_out[k, r - 2] = new[k]
            put_split(lhs, k, at, new[k])
        return 0

    lax.fori_loop(2, LAT - 2, second, 0)
    values_out[...] = blend(lhs[...], whi[2 * LON : 14 * LON], wlo[2 * LON : 14 * LON])
    for k in range(4):
        for j, r in enumerate((1, 2, 13, 14)):
            s1_out[k, j] = s1[k, r]
    for k in range(5):
        for j, r in enumerate((1, 14)):
            faces_out[k, j] = faces[k, r]


def rim_kernel(f, cols, left, right, south, north, s1_in, faces_in, partial, whi, wlo, rim_out, values_out, lhs):
    halo, own = edge_columns(cols, left, right, (south[11], north[11]))
    edge = [swap_middle(h) for h in halo]
    edge1 = [swap_middle(v) for v in relax_columns(halo, own)]

    def field(k, r):
        if r < 0:
            return south[k] if r == -2 else south[5 + k]
        if r >= LAT:
            return north[k] if r == LAT + 1 else north[5 + k]
        return f[k, r]

    s1, faces = {}, {}
    for j, r in enumerate((1, 2, 13, 14)):
        s1[r] = [s1_in[k, j] for k in range(4)]
    for j, r in enumerate((1, 14)):
        low, high, left_face, right_face, scale = (faces_in[k, j] for k in range(5))
        eta = f[4, r]
        faces[r] = (((low, high), (eta + f[4, r - 1], eta + f[4, r + 1]), (left_face, right_face)), scale)
    for r in (-1, 0, LAT - 1, LAT):
        eta = field(4, r)
        faces[r] = faces_of(eta, (depth_pair(eta), (field(4, r - 1), field(4, r + 1)), lon_pair(eta, edge[4], r)))
        centre = [field(k, r) for k in range(4)]
        pairs = [(depth_pair(centre[k]), (field(k, r - 1), field(k, r + 1)), lon_pair(centre[k], edge[k], r)) for k in range(4)]
        s1[r] = relax(centre, pairs, *faces[r], eta, field(5, r))
        if r < 0 or r >= LAT:
            s1[r] = [jnp.where(eta > 0.0, v, 0.0) for v in s1[r]]
    for j, r in enumerate((0, 1, 14, 15)):
        centre = s1[r]
        pairs = [(depth_pair(centre[k]), (s1[r - 1][k], s1[r + 1][k]), lon_pair(centre[k], edge1[k], r)) for k in range(4)]
        t = f[5, r]
        new = relax(centre, pairs, *faces[r], f[4, r], t)
        new.append(advance(t, (depth_pair(t), (field(5, r - 1), field(5, r + 1)), lon_pair(t, edge[5], r)), new))
        for k in range(5):
            rim_out[k, j] = new[k]
            put_split(lhs, k, slice(j * LON, (j + 1) * LON), new[k])
    low, high = slice(0, 2 * LON), slice(14 * LON, 16 * LON)
    values_out[...] = (
        partial[...] + blend(lhs[:, : 2 * LON], whi[low], wlo[low]) + blend(lhs[:, 2 * LON :], whi[high], wlo[high])
    )


def place_kernel(mid, rim, values, table, struck, flow_out, warmth_out, lhs, out, sems):
    n = 5 * DEP
    v = values[...]
    top = v.astype(BF16)
    lhs[0:n] = top
    lhs[n : 2 * n] = (v - top.astype(F32)).astype(BF16)
    copies = []
    for g in range(LAT // 2):
        placed = jnp.dot(lhs[...], table[:, g * 256 : (g + 1) * 256], preferred_element_type=F32)
        merged = placed[:n] + placed[n : 2 * n]
        for h in range(2):
            r = 2 * g + h
            at = slice(h * LON, (h + 1) * LON)
            hit = struck[0:1, r * LON : (r + 1) * LON] > 0.5
            for k in range(5):
                kept = mid[k, r - 2] if 2 <= r < 14 else rim[k, r if r < 2 else r - 12]
                out[k, r] = jnp.where(hit, merged[k * DEP : (k + 1) * DEP, at], kept)
            copies.append(pltpu.make_async_copy(out.at[0:4, r], flow_out.at[:, 0, :, r, :], sems.at[0, r]))
            copies.append(pltpu.make_async_copy(out.at[4, r], warmth_out.at[0, :, r, :], sems.at[1, r]))
            copies[-2].start()
            copies[-1].start()
    for c in copies:
        c.wait()


def shape(*dims, dtype=F32):
    return jax.ShapeDtypeStruct(dims, dtype)


def call(kernel, outs, ins, scratch=(), out_specs=None, flops=0, size=0, aliases=None, limit=None):
    return pl.pallas_call(
        kernel,
        out_shape=outs,
        in_specs=ins,
        out_specs=out_specs or [VMEM] * len(outs),
        scratch_shapes=list(scratch),
        input_output_aliases=aliases or {},
        cost_estimate=pl.CostEstimate(flops=flops, bytes_accessed=size, transcendentals=0),
        compiler_params=pltpu.CompilerParams(vmem_limit_bytes=limit or (32 << 20)),
    )


def in_hbm(x):
    return pltpu.with_memory_space_constraint(x, pltpu.HBM)


def shards(motion, warmth, label, chart, receivers, donors, factors):
    lon, lat = lax.axis_size("lon"), lax.axis_size("lat")
    n, slab = 5 * DEP, (DEP, LON)

    f, cols, up, down, receivers, donors, factors = call(
        stage_kernel,
        [
            shape(6, LAT, *slab), shape(3, *slab), shape(12, *slab), shape(12, *slab),
            shape(1, 512, dtype=jnp.int32), shape(4, 512, dtype=jnp.int32), shape(4, 512),
        ],
        [HBM] * 7,
        [pltpu.VMEM((LAT,) + slab, jnp.int32), pltpu.SMEM((8,), F32), pltpu.SemaphoreType.DMA((4, LAT))],
        size=2 << 20,
    )(*map(in_hbm, (motion, warmth, label, chart, receivers.reshape(1, 512), donors.reshape(4, 512), factors.reshape(4, 512))))

    ahead = lambda n: [(i, i + 1) for i in range(n - 1)]
    back = lambda n: [(i + 1, i) for i in range(n - 1)]
    left = lax.ppermute(cols, "lon", ahead(lon))
    right = lax.ppermute(cols, "lon", back(lon))
    whi, wlo = call(
        weights_kernel,
        [shape(LAT * LON, 512, dtype=BF16), shape(LAT * LON, 512, dtype=BF16)],
        [VMEM, VMEM],
        size=4 << 20,
        flops=20 << 20,
    )(donors, factors)
    up, down = call(
        corners_kernel,
        [shape(12, *slab), shape(12, *slab)],
        [VMEM, VMEM, ANY, ANY, ANY],
        [pltpu.VMEM(slab, F32), pltpu.VMEM(slab, F32), pltpu.SemaphoreType.DMA((2,))],
        out_specs=[ANY, ANY],
        aliases={2: 0, 3: 1},
        size=1 << 16,
    )(left, right, up, down, whi)
    south = lax.ppermute(up, "lat", ahead(lat))
    north = lax.ppermute(down, "lat", back(lat))

    mid, partial, s1, faces = call(
        inner_kernel,
        [shape(5, 12, *slab), shape(n, 512), shape(4, 4, *slab), shape(5, 2, *slab)],
        [VMEM] * 6,
        [
            pltpu.VMEM((4, LAT) + slab, F32),
            pltpu.VMEM((5, LAT) + slab, F32),
            pltpu.VMEM((10,) + slab, F32),
            pltpu.VMEM((2 * n, 12 * LON), BF16),
        ],
        size=8 << 20,
        flops=1 << 30,
    )(f, cols, left, right, whi, wlo)
    rim, values = call(
        rim_kernel,
        [shape(5, 4, *slab), shape(n, 512)],
        [VMEM] * 11,
        [pltpu.VMEM((2 * n, 4 * LON), BF16)],
        size=2 << 20,
        flops=1 << 28,
    )(f, cols, left, right, south, north, s1, faces, partial, whi, wlo)

    mirror = [(p * lon + b, (1 - p) * lon + lon - 1 - b) for p in range(2) for b in range(lon)]
    incoming = lax.ppermute(values, ("panel", "lon"), mirror)

    table, struck = call(
        table_kernel,
        [shape(512, LAT * LON, dtype=BF16), shape(8, LAT * LON)],
        [VMEM],
        size=2 << 20,
        flops=4 << 20,
    )(receivers)

    flow, warm = call(
        place_kernel,
        [shape(4, 1, DEP, LAT, LON), shape(1, DEP, LAT, LON)],
        [VMEM] * 5,
        [pltpu.VMEM((2 * n, 512), BF16), pltpu.VMEM((5, LAT) + slab, F32), pltpu.SemaphoreType.DMA((2, LAT))],
        out_specs=[ANY, ANY],
        size=8 << 20,
        flops=1 << 30,
    )(mid, rim, incoming, table, struck)
    return flow, warm


def solution(mesh):
    field = P("panel", None, "lat", "lon")
    tile = ("panel", "lat", "lon")
    in_specs = (
        P(None, "panel", None, "lat", "lon"),
        field,
        field,
        P(),
        P(*tile, None),
        P(*tile, None, None),
        P(*tile, None, None),
    )
    out_specs = (P(None, "panel", None, "lat", "lon"), field)
    return jax.shard_map(shards, mesh=mesh, in_specs=in_specs, out_specs=out_specs, check_vma=False)
```

```python
import jax
import jax.numpy as jnp
from jax import lax
from jax.experimental import pallas as pl
from jax.experimental.pallas import tpu as pltpu
from jax.sharding import PartitionSpec as P

OMEGA = 0.6
BETA = 0.5
TIME_STEP = 0.05
DIFFUSIVITY = 2.3

F32 = jnp.float32
BF16 = jnp.bfloat16
ANY = pl.BlockSpec(memory_space=pl.ANY)
VMEM = pl.BlockSpec(memory_space=pltpu.VMEM)
HBM = pl.BlockSpec(memory_space=pltpu.HBM)

LAT, DEP, LON = 16, 32, 128


def iota(dim, shape=(DEP, LON)):
    return lax.broadcasted_iota(jnp.int32, shape, dim)


def roll(x, shift, axis):
    return pltpu.roll(x, shift, axis)


def depth_pair(x):
    row = iota(0, x.shape)
    lower = jnp.where(row == 0, 0.0, roll(x, 1, 0))
    upper = jnp.where(row == x.shape[0] - 1, 0.0, roll(x, x.shape[0] - 1, 0))
    return lower, upper


def lon_pair(x, edge, r):
    lane = iota(1, x.shape)
    halo = roll(edge, 122 - 4 * r, 1)
    lower = jnp.where(lane == 0, halo, roll(x, 1, 1))
    upper = jnp.where(lane == LON - 1, halo, roll(x, LON - 1, 1))
    return lower, upper


def swap_middle(c):
    pos = iota(1, c.shape) & 3
    return jnp.where(pos == 1, roll(c, LON - 1, 1), roll(c, 1, 1))


def relax(centre, pairs, faces, scale, eta, warmth):
    out = []
    for c in range(3):
        total = 0.0
        for e in range(3):
            for s in range(2):
                total = total + faces[e][s] * pairs[c][e][s]
        total = total - (pairs[3][c][1] - pairs[3][c][0])
        if c == 0:
            total = total + 4.0 * (warmth - 0.5)
        out.append((1.0 - OMEGA) * centre[c] + total * scale)
    div = 0.0
    for c in range(3):
        div = div + (pairs[c][c][1] - pairs[c][c][0])
    out.append(centre[3] - (0.5 * BETA) * eta * div)
    return out


def odd(axis):
    return lax.rem(lax.axis_index(axis), 2) == 1


def stage_kernel(
    motion, warmth, label, chart, receivers, donors, factors,
    f, cols_out, first_out, second_out, receivers_out, donors_out, factors_out,
    lab, table, sems,
):
    small = [
        pltpu.make_async_copy(chart, table, sems.at[3, 0]),
        pltpu.make_async_copy(receivers, receivers_out, sems.at[3, 1]),
        pltpu.make_async_copy(donors, donors_out, sems.at[3, 2]),
        pltpu.make_async_copy(factors, factors_out, sems.at[3, 3]),
    ]
    scalars, flow = [], []
    for r in range(LAT):
        scalars.append(pltpu.make_async_copy(warmth.at[0, :, r, :], f.at[5, r], sems.at[0, r]))
        scalars.append(pltpu.make_async_copy(label.at[0, :, r, :], lab.at[r], sems.at[1, r]))
        flow.append(pltpu.make_async_copy(motion.at[:, 0, :, r, :], f.at[0:4, r], sems.at[2, r]))
    for c in small[:1] + scalars + flow + small[1:]:
        c.start()
    small[0].wait()

    step = 4
    for start in range(0, LAT, step):
        for c in scalars[2 * start : 2 * (start + step)]:
            c.wait()
        for r in range(start, start + step):
            kind = lab[r]
            exponent = jnp.full(kind.shape, table[0], F32)
            for entry in range(1, 8):
                exponent = jnp.where(kind == entry, table[entry], exponent)
            f[4, r] = jnp.exp(exponent + DIFFUSIVITY * (0.5 - f[5, r]))

    group = iota(1) >> 2

    def pack(q, r, acc):
        first = roll(f[2 * q, r], 4 * r + 2, 1)
        second = roll(f[2 * q + 1, r], 4 * r + 66, 1)
        return jnp.where(group == r, first, jnp.where(group == r + 16, second, acc))

    packed = [jnp.zeros((DEP, LON), F32) for _ in range(3)]
    for start in range(0, LAT, step):
        rows = range(start, start + step)
        for r in rows:
            packed[2] = pack(2, r, packed[2])
        for c in flow[start : start + step]:
            c.wait()
        for r in rows:
            packed[0] = pack(0, r, packed[0])
            packed[1] = pack(1, r, packed[1])
    for q in range(3):
        cols_out[q] = packed[q]
    is_odd = odd("lat")
    for out, above in ((first_out, is_odd), (second_out, jnp.logical_not(is_odd))):
        outer, inner = jnp.where(above, 14, 1), jnp.where(above, 15, 0)
        for k in range(5):
            out[k] = f[k, outer]
        for k in range(6):
            out[5 + k] = f[k, inner]
    for c in small[1:]:
        c.wait()


def from_sides(first, second):
    left_lanes = (iota(1) & 3) < 2
    return [jnp.where(left_lanes == odd("lon"), second[q], first[q]) for q in range(3)]


def corners_kernel(cols_first, cols_second, rows_first, rows_second, _, first_out, second_out, c1, c2, sems):
    group = (iota(1) >> 2) & 15
    pairs = from_sides(cols_first, cols_second)
    up = jnp.where(group == 15, pairs[0], jnp.where(group == 14, roll(pairs[1], 124, 1), roll(pairs[2], 120, 1)))
    down = jnp.where(group == 0, pairs[0], jnp.where(group == 1, roll(pairs[1], 4, 1), roll(pairs[2], 8, 1)))
    c1[...] = jnp.where(odd("lat"), up, down)
    c2[...] = jnp.where(odd("lat"), down, up)
    a = pltpu.make_async_copy(c1, first_out.at[11], sems.at[0])
    b = pltpu.make_async_copy(c2, second_out.at[11], sems.at[1])
    a.start()
    b.start()
    a.wait()
    b.wait()


def weights_kernel(donors, factors, hi, lo):
    def body(i, _):
        cell = iota(0, (32, 512)) + i * 32
        w = jnp.zeros((32, 512), F32)
        for j in range(4):
            w = w + jnp.where(cell == donors[j : j + 1, :], factors[j : j + 1, :], 0.0)
        top = w.astype(BF16)
        at = pl.ds(pl.multiple_of(i * 32, 32), 32)
        hi[at, :] = top
        lo[at, :] = (w - top.astype(F32)).astype(BF16)
        return 0

    lax.fori_loop(0, LAT * LON // 32, body, 0)


def table_kernel(receivers, table, struck):
    columns = []
    for b in range(4):
        row = receivers[:, b * 128 : (b + 1) * 128].astype(F32)
        columns.append(jnp.broadcast_to(row, (128, 128)).T.astype(jnp.int32))

    def body(i, _):
        cell = iota(1, (128, LON)) + i * LON
        at = pl.ds(pl.multiple_of(i * LON, LON), LON)
        total = jnp.zeros((1, LON), F32)
        for b in range(4):
            hit = jnp.where(cell == columns[b], 1.0, 0.0)
            table[b * 128 : (b + 1) * 128, at] = hit.astype(BF16)
            total = total + jnp.sum(hit, axis=0, keepdims=True)
        struck[:, at] = jnp.broadcast_to(total, (8, LON))
        return 0

    lax.fori_loop(0, LAT, body, 0)


def edge_columns(cols, first, second, corners):
    lane = iota(1)
    group = lane >> 2
    sides = from_sides(first, second)
    halo, own = [], []
    for k in range(6):
        q, h = k // 2, k % 2
        c = roll(sides[q], 4 + 64 * h, 1)
        low = high = 0.0
        if corners is not None:
            low = roll(corners[0], (68 + 64 * h + 4 * q) % 128, 1)
            high = roll(corners[1], (68 + 64 * h - 4 * q) % 128, 1)
        halo.append(jnp.where(group == 0, low, jnp.where(group == 17, high, c)))
        own.append(roll(cols[q], 4 + 64 * h, 1))
    return halo, own


def relax_columns(halo, own):
    middle = (iota(1) & 3) == 1

    def pairs_of(k):
        c, o = halo[k], own[k]
        lower = jnp.where(middle, roll(c, 1, 1), roll(o, 1, 1))
        upper = jnp.where(middle, roll(o, LON - 1, 1), roll(c, LON - 1, 1))
        return depth_pair(c), (roll(c, 4, 1), roll(c, LON - 4, 1)), (lower, upper)

    faces, scale = faces_of(halo[4], pairs_of(4))
    inside = halo[4] > 0.0
    new = relax(halo[:4], [pairs_of(k) for k in range(4)], faces, scale, halo[4], halo[5])
    return [jnp.where(inside, v, 0.0) for v in new]


def faces_of(eta, pairs):
    faces = [[eta + n for n in pair] for pair in pairs]
    diagonal = faces[0][0] + faces[0][1] + faces[1][0] + faces[1][1] + faces[2][0] + faces[2][1]
    return faces, OMEGA / jnp.where(diagonal > 0.0, diagonal, 1.0)


def advance(t, pairs, speed):
    change = 0.0
    for e, (lower, upper) in enumerate(pairs):
        change = (
            change
            - jnp.maximum(speed[e], 0.0) * (t - lower)
            - jnp.minimum(speed[e], 0.0) * (upper - t)
            + (upper + lower - 2.0 * t)
        )
    return t + TIME_STEP * change


def blend(lhs, hi, lo):
    n = 5 * DEP
    wide = jnp.dot(lhs, hi, preferred_element_type=F32)
    return wide[:n] + wide[n:] + jnp.dot(lhs[:n], lo, preferred_element_type=F32)


def put_split(lhs, k, at, value):
    top = value.astype(BF16)
    lhs[k * DEP : (k + 1) * DEP, at] = top
    lhs[(5 + k) * DEP : (6 + k) * DEP, at] = (value - top.astype(F32)).astype(BF16)


def inner_kernel(f, cols, cols_first, cols_second, whi, wlo, mid_out, values_out, s1_out, faces_out, s1, faces, edge, lhs):
    halo, own = edge_columns(cols, cols_first, cols_second, None)
    for k in range(6):
        edge[k] = swap_middle(halo[k])
    for k, v in enumerate(relax_columns(halo, own)):
        edge[6 + k] = swap_middle(v)

    def first(r, _):
        eta = f[4, r]
        both, scale = faces_of(eta, (depth_pair(eta), (f[4, r - 1], f[4, r + 1]), lon_pair(eta, edge[4], r)))
        for j, v in enumerate((both[0][0], both[0][1], both[2][0], both[2][1], scale)):
            faces[j, r] = v
        centre = [f[k, r] for k in range(4)]
        pairs = [(depth_pair(centre[k]), (f[k, r - 1], f[k, r + 1]), lon_pair(centre[k], edge[k], r)) for k in range(4)]
        for k, v in enumerate(relax(centre, pairs, both, scale, eta, f[5, r])):
            s1[k, r] = v
        return 0

    lax.fori_loop(1, LAT - 1, first, 0)

    def second(r, _):
        eta = f[4, r]
        both = ((faces[0, r], faces[1, r]), (eta + f[4, r - 1], eta + f[4, r + 1]), (faces[2, r], faces[3, r]))
        centre = [s1[k, r] for k in range(4)]
        pairs = [(depth_pair(centre[k]), (s1[k, r - 1], s1[k, r + 1]), lon_pair(centre[k], edge[6 + k], r)) for k in range(4)]
        t = f[5, r]
        new = relax(centre, pairs, both, faces[4, r], eta, t)
        new.append(advance(t, (depth_pair(t), (f[5, r - 1], f[5, r + 1]), lon_pair(t, edge[5], r)), new))
        at = pl.ds(pl.multiple_of((r - 2) * LON, LON), LON)
        for k in range(5):
            mid_out[k, r - 2] = new[k]
            put_split(lhs, k, at, new[k])
        return 0

    lax.fori_loop(2, LAT - 2, second, 0)
    values_out[...] = blend(lhs[...], whi[2 * LON : 14 * LON], wlo[2 * LON : 14 * LON])
    for k in range(4):
        for j, r in enumerate((1, 2, 13, 14)):
            s1_out[k, j] = s1[k, r]
    for k in range(5):
        for j, r in enumerate((1, 14)):
            faces_out[k, j] = faces[k, r]


def rim_kernel(f, cols, cols_first, cols_second, rows_first, rows_second, s1_in, faces_in, partial, whi, wlo, rim_out, values_out, lhs):
    is_odd = odd("lat")
    south = lambda i: jnp.where(is_odd, rows_second[i], rows_first[i])
    north = lambda i: jnp.where(is_odd, rows_first[i], rows_second[i])
    halo, own = edge_columns(cols, cols_first, cols_second, (south(11), north(11)))
    edge = [swap_middle(h) for h in halo]
    edge1 = [swap_middle(v) for v in relax_columns(halo, own)]

    def field(k, r):
        if r < 0:
            return south(k if r == -2 else 5 + k)
        if r >= LAT:
            return north(k if r == LAT + 1 else 5 + k)
        return f[k, r]

    s1, faces = {}, {}
    for j, r in enumerate((1, 2, 13, 14)):
        s1[r] = [s1_in[k, j] for k in range(4)]
    for j, r in enumerate((1, 14)):
        low, high, left_face, right_face, scale = (faces_in[k, j] for k in range(5))
        eta = f[4, r]
        faces[r] = (((low, high), (eta + f[4, r - 1], eta + f[4, r + 1]), (left_face, right_face)), scale)
    for r in (-1, 0, LAT - 1, LAT):
        eta = field(4, r)
        faces[r] = faces_of(eta, (depth_pair(eta), (field(4, r - 1), field(4, r + 1)), lon_pair(eta, edge[4], r)))
        centre = [field(k, r) for k in range(4)]
        pairs = [(depth_pair(centre[k]), (field(k, r - 1), field(k, r + 1)), lon_pair(centre[k], edge[k], r)) for k in range(4)]
        s1[r] = relax(centre, pairs, *faces[r], eta, field(5, r))
        if r < 0 or r >= LAT:
            s1[r] = [jnp.where(eta > 0.0, v, 0.0) for v in s1[r]]
    for j, r in enumerate((0, 1, 14, 15)):
        centre = s1[r]
        pairs = [(depth_pair(centre[k]), (s1[r - 1][k], s1[r + 1][k]), lon_pair(centre[k], edge1[k], r)) for k in range(4)]
        t = f[5, r]
        new = relax(centre, pairs, *faces[r], f[4, r], t)
        new.append(advance(t, (depth_pair(t), (field(5, r - 1), field(5, r + 1)), lon_pair(t, edge[5], r)), new))
        for k in range(5):
            rim_out[k, j] = new[k]
            put_split(lhs, k, slice(j * LON, (j + 1) * LON), new[k])
    low, high = slice(0, 2 * LON), slice(14 * LON, 16 * LON)
    values_out[...] = (
        partial[...] + blend(lhs[:, : 2 * LON], whi[low], wlo[low]) + blend(lhs[:, 2 * LON :], whi[high], wlo[high])
    )


def place_kernel(mid, rim, values, table, struck, flow_out, warmth_out, lhs, out, sems):
    n = 5 * DEP
    v = values[...]
    top = v.astype(BF16)
    lhs[0:n] = top
    lhs[n : 2 * n] = (v - top.astype(F32)).astype(BF16)
    copies = []
    half = LAT // 2
    for g in range(2):
        placed = jnp.dot(lhs[...], table[:, g * half * LON : (g + 1) * half * LON], preferred_element_type=F32)
        merged = placed[:n] + placed[n : 2 * n]
        for h in range(half):
            r = g * half + h
            hit = struck[0:1, r * LON : (r + 1) * LON] > 0.5
            for k in range(5):
                kept = mid[k, r - 2] if 2 <= r < 14 else rim[k, r if r < 2 else r - 12]
                out[k, r] = jnp.where(hit, merged[k * DEP : (k + 1) * DEP, h * LON : (h + 1) * LON], kept)
        for r in range(g * half, (g + 1) * half):
            copies.append(pltpu.make_async_copy(out.at[0:4, r], flow_out.at[:, 0, :, r, :], sems.at[0, r]))
            copies.append(pltpu.make_async_copy(out.at[4, r], warmth_out.at[0, :, r, :], sems.at[1, r]))
            copies[-2].start()
            copies[-1].start()
    for c in copies:
        c.wait()


def shape(*dims, dtype=F32):
    return jax.ShapeDtypeStruct(dims, dtype)


def call(kernel, outs, ins, scratch=(), out_specs=None, flops=0, size=0, aliases=None, limit=None):
    return pl.pallas_call(
        kernel,
        out_shape=outs,
        in_specs=ins,
        out_specs=out_specs or [VMEM] * len(outs),
        scratch_shapes=list(scratch),
        input_output_aliases=aliases or {},
        cost_estimate=pl.CostEstimate(flops=flops, bytes_accessed=size, transcendentals=0),
        compiler_params=pltpu.CompilerParams(vmem_limit_bytes=limit or (32 << 20)),
    )


def in_hbm(x):
    return pltpu.with_memory_space_constraint(x, pltpu.HBM)


def shards(motion, warmth, label, chart, receivers, donors, factors):
    lon, lat = lax.axis_size("lon"), lax.axis_size("lat")
    n, slab = 5 * DEP, (DEP, LON)

    f, cols, rows_first, rows_second, receivers, donors, factors = call(
        stage_kernel,
        [
            shape(6, LAT, *slab), shape(3, *slab), shape(12, *slab), shape(12, *slab),
            shape(1, 512, dtype=jnp.int32), shape(4, 512, dtype=jnp.int32), shape(4, 512),
        ],
        [HBM] * 7,
        [pltpu.VMEM((LAT,) + slab, jnp.int32), pltpu.SMEM((8,), F32), pltpu.SemaphoreType.DMA((4, LAT))],
        size=2 << 20,
    )(*map(in_hbm, (motion, warmth, label, chart, receivers.reshape(1, 512), donors.reshape(4, 512), factors.reshape(4, 512))))

    swap = lambda n, start: [(i + j, i + 1 - j) for i in range(start, n - 1, 2) for j in range(2)]
    cols_first = lax.ppermute(cols, "lon", swap(lon, 1))
    cols_second = lax.ppermute(cols, "lon", swap(lon, 0))
    whi, wlo = call(
        weights_kernel,
        [shape(LAT * LON, 512, dtype=BF16), shape(LAT * LON, 512, dtype=BF16)],
        [VMEM, VMEM],
        size=4 << 20,
        flops=20 << 20,
    )(donors, factors)
    rows_first, rows_second = call(
        corners_kernel,
        [shape(12, *slab), shape(12, *slab)],
        [VMEM, VMEM, ANY, ANY, ANY],
        [pltpu.VMEM(slab, F32), pltpu.VMEM(slab, F32), pltpu.SemaphoreType.DMA((2,))],
        out_specs=[ANY, ANY],
        aliases={2: 0, 3: 1},
        size=1 << 16,
    )(cols_first, cols_second, rows_first, rows_second, whi)
    rows_first = lax.ppermute(rows_first, "lat", swap(lat, 1))
    rows_second = lax.ppermute(rows_second, "lat", swap(lat, 0))

    mid, partial, s1, faces = call(
        inner_kernel,
        [shape(5, 12, *slab), shape(n, 512), shape(4, 4, *slab), shape(5, 2, *slab)],
        [VMEM] * 6,
        [
            pltpu.VMEM((4, LAT) + slab, F32),
            pltpu.VMEM((5, LAT) + slab, F32),
            pltpu.VMEM((10,) + slab, F32),
            pltpu.VMEM((2 * n, 12 * LON), BF16),
        ],
        size=8 << 20,
        flops=1 << 30,
    )(f, cols, cols_first, cols_second, whi, wlo)
    rim, values = call(
        rim_kernel,
        [shape(5, 4, *slab), shape(n, 512)],
        [VMEM] * 11,
        [pltpu.VMEM((2 * n, 4 * LON), BF16)],
        size=2 << 20,
        flops=1 << 28,
    )(f, cols, cols_first, cols_second, rows_first, rows_second, s1, faces, partial, whi, wlo)

    mirror = [(p * lon + b, (1 - p) * lon + lon - 1 - b) for p in range(2) for b in range(lon)]
    incoming = lax.ppermute(values, ("panel", "lon"), mirror)

    table, struck = call(
        table_kernel,
        [shape(512, LAT * LON, dtype=BF16), shape(8, LAT * LON)],
        [VMEM],
        size=2 << 20,
        flops=4 << 20,
    )(receivers)

    flow, warm = call(
        place_kernel,
        [shape(4, 1, DEP, LAT, LON), shape(1, DEP, LAT, LON)],
        [VMEM] * 5,
        [pltpu.VMEM((2 * n, 512), BF16), pltpu.VMEM((5, LAT) + slab, F32), pltpu.SemaphoreType.DMA((2, LAT))],
        out_specs=[ANY, ANY],
        size=8 << 20,
        flops=1 << 30,
    )(mid, rim, incoming, table, struck)
    return flow, warm


def solution(mesh):
    field = P("panel", None, "lat", "lon")
    tile = ("panel", "lat", "lon")
    in_specs = (
        P(None, "panel", None, "lat", "lon"),
        field,
        field,
        P(),
        P(*tile, None),
        P(*tile, None, None),
        P(*tile, None, None),
    )
    out_specs = (P(None, "panel", None, "lat", "lon"), field)
    return jax.shard_map(shards, mesh=mesh, in_specs=in_specs, out_specs=out_specs, check_vma=False)
```

```python
import jax
import jax.numpy as jnp
from jax import lax
from jax.experimental import pallas as pl
from jax.experimental.pallas import tpu as pltpu
from jax.sharding import PartitionSpec as P

OMEGA = 0.6
BETA = 0.5
TIME_STEP = 0.05
DIFFUSIVITY = 2.3

F32 = jnp.float32
BF16 = jnp.bfloat16
ANY = pl.BlockSpec(memory_space=pl.ANY)
VMEM = pl.BlockSpec(memory_space=pltpu.VMEM)
HBM = pl.BlockSpec(memory_space=pltpu.HBM)

LAT, DEP, LON = 16, 32, 128


def iota(dim, shape=(DEP, LON)):
    return lax.broadcasted_iota(jnp.int32, shape, dim)


def roll(x, shift, axis):
    return pltpu.roll(x, shift, axis)


def depth_pair(x):
    row = iota(0, x.shape)
    lower = jnp.where(row == 0, 0.0, roll(x, 1, 0))
    upper = jnp.where(row == x.shape[0] - 1, 0.0, roll(x, x.shape[0] - 1, 0))
    return lower, upper


def lon_pair(x, edge, r):
    return beside(x, roll(edge, 122 - 4 * r, 1))


def beside(x, halo):
    lane = iota(1, x.shape)
    lower = jnp.where(lane == 0, halo, roll(x, 1, 1))
    upper = jnp.where(lane == LON - 1, halo, roll(x, LON - 1, 1))
    return lower, upper


def swap_middle(c):
    pos = iota(1, c.shape) & 3
    return jnp.where(pos == 1, roll(c, LON - 1, 1), roll(c, 1, 1))


def relax(centre, pairs, faces, scale, eta, warmth):
    out = []
    for c in range(3):
        total = 0.0
        for e in range(3):
            for s in range(2):
                total = total + faces[e][s] * pairs[c][e][s]
        total = total - (pairs[3][c][1] - pairs[3][c][0])
        if c == 0:
            total = total + 4.0 * (warmth - 0.5)
        out.append((1.0 - OMEGA) * centre[c] + total * scale)
    div = 0.0
    for c in range(3):
        div = div + (pairs[c][c][1] - pairs[c][c][0])
    out.append(centre[3] - (0.5 * BETA) * eta * div)
    return out


def odd(axis):
    return lax.rem(lax.axis_index(axis), 2) == 1


def middle_of(lon):
    return range(lon // 4, lon - lon // 4)


def first_above():
    b, middle = lax.axis_index("lon"), middle_of(lax.axis_size("lon"))
    return odd("lat") == jnp.logical_and(b >= middle.start, b < middle.stop)


def stage_kernel(
    motion, warmth, label, chart, receivers, donors, factors,
    f, cols_out, side_first_out, side_second_out, first_out, second_out, receivers_out, donors_out, factors_out,
    lab, table, sems,
):
    small = [
        pltpu.make_async_copy(chart, table, sems.at[3, 0]),
        pltpu.make_async_copy(receivers, receivers_out, sems.at[3, 1]),
        pltpu.make_async_copy(donors, donors_out, sems.at[3, 2]),
        pltpu.make_async_copy(factors, factors_out, sems.at[3, 3]),
    ]
    scalars, flow = [], []
    for r in range(LAT):
        scalars.append(pltpu.make_async_copy(warmth.at[0, :, r, :], f.at[5, r], sems.at[0, r]))
        scalars.append(pltpu.make_async_copy(label.at[0, :, r, :], lab.at[r], sems.at[1, r]))
        flow.append(pltpu.make_async_copy(motion.at[:, 0, :, r, :], f.at[0:4, r], sems.at[2, r]))
    for c in small[:1] + scalars + flow + small[1:]:
        c.start()
    small[0].wait()

    step = 4
    for start in range(0, LAT, step):
        for c in scalars[2 * start : 2 * (start + step)]:
            c.wait()
        for r in range(start, start + step):
            kind = lab[r]
            exponent = jnp.full(kind.shape, table[0], F32)
            for entry in range(1, 8):
                exponent = jnp.where(kind == entry, table[entry], exponent)
            f[4, r] = jnp.exp(exponent + DIFFUSIVITY * (0.5 - f[5, r]))

    group = iota(1) >> 2

    def pack(q, r, acc):
        first = roll(f[2 * q, r], 4 * r + 2, 1)
        second = roll(f[2 * q + 1, r], 4 * r + 66, 1)
        return jnp.where(group == r, first, jnp.where(group == r + 16, second, acc))

    packed = [jnp.zeros((DEP, LON), F32) for _ in range(3)]
    for start in range(0, LAT, step):
        rows = range(start, start + step)
        for r in rows:
            packed[2] = pack(2, r, packed[2])
        for c in flow[start : start + step]:
            c.wait()
        for r in rows:
            packed[0] = pack(0, r, packed[0])
            packed[1] = pack(1, r, packed[1])
    for q in range(3):
        cols_out[q] = packed[q]
    to_right, to_left = side_columns(packed, 0), side_columns(packed, 2)
    for i in range(2):
        rows = slice(0, DEP) if i == 0 else slice(DEP, DEP + DEP // 2)
        side_first_out[rows] = jnp.where(odd("lon"), to_right[i], to_left[i])
        side_second_out[rows] = jnp.where(odd("lon"), to_left[i], to_right[i])
    is_above = first_above()
    for out, above in ((first_out, is_above), (second_out, jnp.logical_not(is_above))):
        outer, inner = jnp.where(above, 14, 1), jnp.where(above, 15, 0)
        for k in range(5):
            out[block(k)] = f[k, outer]
        for k in range(6):
            out[block(5 + k)] = f[k, inner]
    for c in small[1:]:
        c.wait()


def block(i):
    return slice(i * DEP, (i + 1) * DEP)


def side_columns(packed, start):
    low_lanes = (iota(1) & 3) < 2
    low = [roll(p, (LON - start) % LON, 1) if start else p for p in packed]
    high = [roll(p, (2 - start) % LON, 1) if start != 2 else p for p in packed]
    half = DEP // 2
    return jnp.where(low_lanes, low[0], high[1]), jnp.where(low_lanes[:half], low[2][:half], high[2][half:])


def by_side(first, second):
    is_odd = odd("lon")
    return jnp.where(is_odd, second[...], first[...]), jnp.where(is_odd, first[...], second[...])


def from_sides(first, second):
    left_lanes = (iota(1) & 3) < 2
    left, right = by_side(first, second)
    l01, l2, r01, r2 = left[:DEP], left[DEP:], right[:DEP], right[DEP:]
    lefts = (l01, roll(l01, LON - 2, 1), jnp.concatenate([l2, roll(l2, LON - 2, 1)], axis=0))
    rights = (roll(r01, 2, 1), r01, jnp.concatenate([roll(r2, 2, 1), r2], axis=0))
    return [jnp.where(left_lanes, a, b) for a, b in zip(lefts, rights)]


CORNERS = slice(11 * DEP, 11 * DEP + 8)


def corners_kernel(cols_first, cols_second, rows_first, rows_second, _, first_out, second_out, c1, c2, sems):
    lane = iota(1, (8, LON))
    left_lanes, group = (lane & 3) < 2, (lane >> 2) & 15
    left, right = by_side(cols_first, cols_second)
    up = down = jnp.zeros((8, LON), F32)
    for j in range(4):
        for q in range(3):
            if q < 2:
                rows, from_left, from_right = slice(8 * j, 8 * j + 8), (0, -2)[q], (2, 0)[q]
            else:
                start = DEP + 8 * (j % 2)
                rows, from_left, from_right = slice(start, start + 8), (0, -2)[j // 2], (2, 0)[j // 2]
            move = 4 * q + 16 * j
            put = lambda x, shift: roll(x[rows], shift % LON, 1) if shift % LON else x[rows]
            to_up = jnp.where(left_lanes, put(left, from_left - move), put(right, from_right - move))
            to_down = jnp.where(left_lanes, put(left, from_left + move), put(right, from_right + move))
            up = jnp.where(group == 15 - q - 4 * j, to_up, up)
            down = jnp.where(group == q + 4 * j, to_down, down)
    c1[...] = jnp.where(first_above(), up, down)
    c2[...] = jnp.where(first_above(), down, up)
    a = pltpu.make_async_copy(c1, first_out.at[CORNERS], sems.at[0])
    b = pltpu.make_async_copy(c2, second_out.at[CORNERS], sems.at[1])
    a.start()
    b.start()
    a.wait()
    b.wait()


def weights_kernel(donors, factors, hi, lo):
    def body(i, _):
        cell = iota(0, (32, 512)) + i * 32
        w = jnp.zeros((32, 512), F32)
        for j in range(4):
            w = w + jnp.where(cell == donors[j : j + 1, :], factors[j : j + 1, :], 0.0)
        top = w.astype(BF16)
        at = pl.ds(pl.multiple_of(i * 32, 32), 32)
        hi[at, :] = top
        lo[at, :] = (w - top.astype(F32)).astype(BF16)
        return 0

    lax.fori_loop(0, LAT * LON // 32, body, 0)


def table_kernel(receivers, table, struck):
    columns = []
    for b in range(4):
        row = receivers[:, b * 128 : (b + 1) * 128].astype(F32)
        columns.append(jnp.broadcast_to(row, (128, 128)).T.astype(jnp.int32))

    def body(i, _):
        cell = iota(1, (128, LON)) + i * LON
        at = pl.ds(pl.multiple_of(i * LON, LON), LON)
        total = jnp.zeros((1, LON), F32)
        for b in range(4):
            hit = jnp.where(cell == columns[b], 1.0, 0.0)
            table[b * 128 : (b + 1) * 128, at] = hit.astype(BF16)
            total = total + jnp.sum(hit, axis=0, keepdims=True)
        struck[:, at] = jnp.broadcast_to(total, (8, LON))
        return 0

    lax.fori_loop(0, LAT, body, 0)


def edge_columns(cols, first, second):
    sides = from_sides(first, second)
    halo, own = [], []
    for k in range(6):
        q, h = k // 2, k % 2
        halo.append(roll(sides[q], 4 + 64 * h, 1))
        own.append(roll(cols[q], 4 + 64 * h, 1))
    return halo, own


def corner_columns(packed, k, up, lane):
    q, h = k // 2, k % 2
    parts = []
    for j in range(4):
        start = 64 * h + (60 - 4 * q - 16 * j if up else 4 * q + 16 * j)
        parts.append(roll(packed, (lane - start) % LON, 1))
    return jnp.concatenate(parts, axis=0)


def relax_columns(halo, own):
    middle = (iota(1) & 3) == 1

    def pairs_of(k):
        c, o = halo[k], own[k]
        lower = jnp.where(middle, roll(c, 1, 1), roll(o, 1, 1))
        upper = jnp.where(middle, roll(o, LON - 1, 1), roll(c, LON - 1, 1))
        return depth_pair(c), (roll(c, 4, 1), roll(c, LON - 4, 1)), (lower, upper)

    faces, scale = faces_of(halo[4], pairs_of(4))
    inside = halo[4] > 0.0
    new = relax(halo[:4], [pairs_of(k) for k in range(4)], faces, scale, halo[4], halo[5])
    return [jnp.where(inside, v, 0.0) for v in new]


def faces_of(eta, pairs):
    faces = [[eta + n for n in pair] for pair in pairs]
    diagonal = faces[0][0] + faces[0][1] + faces[1][0] + faces[1][1] + faces[2][0] + faces[2][1]
    return faces, OMEGA / jnp.where(diagonal > 0.0, diagonal, 1.0)


def advance(t, pairs, speed):
    change = 0.0
    for e, (lower, upper) in enumerate(pairs):
        change = (
            change
            - jnp.maximum(speed[e], 0.0) * (t - lower)
            - jnp.minimum(speed[e], 0.0) * (upper - t)
            + (upper + lower - 2.0 * t)
        )
    return t + TIME_STEP * change


def blend(lhs, hi, lo):
    n = 5 * DEP
    wide = jnp.dot(lhs, hi, preferred_element_type=F32)
    return wide[:n] + wide[n:] + jnp.dot(lhs[:n], lo, preferred_element_type=F32)


def put_split(lhs, k, at, value):
    top = value.astype(BF16)
    lhs[k * DEP : (k + 1) * DEP, at] = top
    lhs[(5 + k) * DEP : (6 + k) * DEP, at] = (value - top.astype(F32)).astype(BF16)


def inner_kernel(f, cols, cols_first, cols_second, whi, wlo, mid_out, values_out, s1_out, faces_out, edges_out, s1, faces, edge, lhs):
    halo, own = edge_columns(cols, cols_first, cols_second)
    for k in range(6):
        edge[k] = swap_middle(halo[k])
        edges_out[k], edges_out[6 + k], edges_out[12 + k] = halo[k], own[k], edge[k]
    for k, v in enumerate(relax_columns(halo, own)):
        edge[6 + k] = swap_middle(v)

    def first(r, _):
        eta = f[4, r]
        both, scale = faces_of(eta, (depth_pair(eta), (f[4, r - 1], f[4, r + 1]), lon_pair(eta, edge[4], r)))
        for j, v in enumerate((both[0][0], both[0][1], both[2][0], both[2][1], scale)):
            faces[j, r] = v
        centre = [f[k, r] for k in range(4)]
        pairs = [(depth_pair(centre[k]), (f[k, r - 1], f[k, r + 1]), lon_pair(centre[k], edge[k], r)) for k in range(4)]
        for k, v in enumerate(relax(centre, pairs, both, scale, eta, f[5, r])):
            s1[k, r] = v
        return 0

    lax.fori_loop(1, LAT - 1, first, 0, unroll=2)

    def second(r, _):
        eta = f[4, r]
        both = ((faces[0, r], faces[1, r]), (eta + f[4, r - 1], eta + f[4, r + 1]), (faces[2, r], faces[3, r]))
        centre = [s1[k, r] for k in range(4)]
        pairs = [(depth_pair(centre[k]), (s1[k, r - 1], s1[k, r + 1]), lon_pair(centre[k], edge[6 + k], r)) for k in range(4)]
        t = f[5, r]
        new = relax(centre, pairs, both, faces[4, r], eta, t)
        new.append(advance(t, (depth_pair(t), (f[5, r - 1], f[5, r + 1]), lon_pair(t, edge[5], r)), new))
        at = pl.ds(pl.multiple_of((r - 2) * LON, LON), LON)
        for k in range(5):
            mid_out[k, r - 2] = new[k]
            put_split(lhs, k, at, new[k])
        return 0

    lax.fori_loop(2, LAT - 2, second, 0, unroll=2)
    values_out[...] = blend(lhs[...], whi[2 * LON : 14 * LON], wlo[2 * LON : 14 * LON])
    for k in range(4):
        for j, r in enumerate((1, 2, 13, 14)):
            s1_out[k, j] = s1[k, r]
    for k in range(5):
        for j, r in enumerate((1, 14)):
            faces_out[k, j] = faces[k, r]


def rim_kernel(f, edges, rows_first, rows_second, s1_in, faces_in, partial, whi, wlo, rim_out, values_out, lhs):
    is_above = first_above()
    south = lambda at: jnp.where(is_above, rows_second[at], rows_first[at])
    north = lambda at: jnp.where(is_above, rows_first[at], rows_second[at])
    low, high = south(CORNERS), north(CORNERS)
    group = iota(1) >> 2
    halo = []
    for k in range(6):
        c = edges[k]
        if k < 5:
            c = jnp.where(group == 0, corner_columns(low, k, True, 0), jnp.where(group == LAT + 1, corner_columns(high, k, False, 4 * LAT + 4), c))
        halo.append(c)
    edge1 = [swap_middle(v) for v in relax_columns(halo, [edges[6 + k] for k in range(6)])]
    low_edge, high_edge = swap_middle(low), swap_middle(high)

    def edge(k, r):
        if r < 0:
            return corner_columns(low_edge, k, True, LON - 2)
        if r >= LAT:
            return corner_columns(high_edge, k, False, LON - 2)
        return roll(edges[12 + k], 122 - 4 * r, 1)

    def field(k, r):
        if r < 0:
            return south(block(k if r == -2 else 5 + k))
        if r >= LAT:
            return north(block(k if r == LAT + 1 else 5 + k))
        return f[k, r]

    s1, faces = {}, {}
    for j, r in enumerate((1, 2, 13, 14)):
        s1[r] = [s1_in[k, j] for k in range(4)]
    for j, r in enumerate((1, 14)):
        below, above, left_face, right_face, scale = (faces_in[k, j] for k in range(5))
        eta = f[4, r]
        faces[r] = (((below, above), (eta + f[4, r - 1], eta + f[4, r + 1]), (left_face, right_face)), scale)
    for r in (-1, 0, LAT - 1, LAT):
        eta = field(4, r)
        faces[r] = faces_of(eta, (depth_pair(eta), (field(4, r - 1), field(4, r + 1)), beside(eta, edge(4, r))))
        centre = [field(k, r) for k in range(4)]
        pairs = [(depth_pair(centre[k]), (field(k, r - 1), field(k, r + 1)), beside(centre[k], edge(k, r))) for k in range(4)]
        s1[r] = relax(centre, pairs, *faces[r], eta, field(5, r))
        if r < 0 or r >= LAT:
            s1[r] = [jnp.where(eta > 0.0, v, 0.0) for v in s1[r]]
    for j, r in enumerate((0, 1, 14, 15)):
        centre = s1[r]
        pairs = [(depth_pair(centre[k]), (s1[r - 1][k], s1[r + 1][k]), lon_pair(centre[k], edge1[k], r)) for k in range(4)]
        t = f[5, r]
        new = relax(centre, pairs, *faces[r], f[4, r], t)
        new.append(advance(t, (depth_pair(t), (field(5, r - 1), field(5, r + 1)), beside(t, edge(5, r))), new))
        for k in range(5):
            rim_out[k, j] = new[k]
            put_split(lhs, k, slice(j * LON, (j + 1) * LON), new[k])
    low, high = slice(0, 2 * LON), slice(14 * LON, 16 * LON)
    values_out[...] = (
        partial[...] + blend(lhs[:, : 2 * LON], whi[low], wlo[low]) + blend(lhs[:, 2 * LON :], whi[high], wlo[high])
    )


def place_kernel(mid, rim, values, table, struck, flow_out, warmth_out, lhs, out, sems):
    n = 5 * DEP
    v = values[...]
    top = v.astype(BF16)
    lhs[0:n] = top
    lhs[n : 2 * n] = (v - top.astype(F32)).astype(BF16)
    copies = []
    half = LAT // 2
    for g in range(2):
        placed = jnp.dot(lhs[...], table[:, g * half * LON : (g + 1) * half * LON], preferred_element_type=F32)
        merged = placed[:n] + placed[n : 2 * n]
        for h in range(half):
            r = g * half + h
            hit = struck[0:1, r * LON : (r + 1) * LON] > 0.5
            for k in range(5):
                kept = mid[k, r - 2] if 2 <= r < 14 else rim[k, r if r < 2 else r - 12]
                out[k, r] = jnp.where(hit, merged[k * DEP : (k + 1) * DEP, h * LON : (h + 1) * LON], kept)
        for r in range(g * half, (g + 1) * half):
            copies.append(pltpu.make_async_copy(out.at[0:4, r], flow_out.at[:, 0, :, r, :], sems.at[0, r]))
            copies.append(pltpu.make_async_copy(out.at[4, r], warmth_out.at[0, :, r, :], sems.at[1, r]))
            copies[-2].start()
            copies[-1].start()
    for c in copies:
        c.wait()


def shape(*dims, dtype=F32):
    return jax.ShapeDtypeStruct(dims, dtype)


def call(kernel, outs, ins, scratch=(), out_specs=None, flops=0, size=0, aliases=None, limit=None):
    return pl.pallas_call(
        kernel,
        out_shape=outs,
        in_specs=ins,
        out_specs=out_specs or [VMEM] * len(outs),
        scratch_shapes=list(scratch),
        input_output_aliases=aliases or {},
        cost_estimate=pl.CostEstimate(flops=flops, bytes_accessed=size, transcendentals=0),
        compiler_params=pltpu.CompilerParams(vmem_limit_bytes=limit or (32 << 20)),
    )


def in_hbm(x):
    return pltpu.with_memory_space_constraint(x, pltpu.HBM)


def shards(motion, warmth, label, chart, receivers, donors, factors):
    lon, lat = lax.axis_size("lon"), lax.axis_size("lat")
    n, slab = 5 * DEP, (DEP, LON)

    sides, rows = shape(DEP + DEP // 2, LON), shape(11 * DEP + 8, LON)
    f, cols, side_first, side_second, rows_first, rows_second, receivers, donors, factors = call(
        stage_kernel,
        [
            shape(6, LAT, *slab), shape(3, *slab), sides, sides, rows, rows,
            shape(1, 512, dtype=jnp.int32), shape(4, 512, dtype=jnp.int32), shape(4, 512),
        ],
        [HBM] * 7,
        [pltpu.VMEM((LAT,) + slab, jnp.int32), pltpu.SMEM((8,), F32), pltpu.SemaphoreType.DMA((4, LAT))],
        size=2 << 20,
    )(*map(in_hbm, (motion, warmth, label, chart, receivers.reshape(1, 512), donors.reshape(4, 512), factors.reshape(4, 512))))

    swap = lambda n, start: [(i + j, i + 1 - j) for i in range(start, n - 1, 2) for j in range(2)]
    cols_first = lax.ppermute(side_first, "lon", swap(lon, 1))
    cols_second = lax.ppermute(side_second, "lon", swap(lon, 0))
    whi, wlo = call(
        weights_kernel,
        [shape(LAT * LON, 512, dtype=BF16), shape(LAT * LON, 512, dtype=BF16)],
        [VMEM, VMEM],
        size=4 << 20,
        flops=20 << 20,
    )(donors, factors)
    rows_first, rows_second = call(
        corners_kernel,
        [rows, rows],
        [VMEM, VMEM, ANY, ANY, ANY],
        [pltpu.VMEM((8, LON), F32), pltpu.VMEM((8, LON), F32), pltpu.SemaphoreType.DMA((2,))],
        out_specs=[ANY, ANY],
        aliases={2: 0, 3: 1},
        size=1 << 16,
    )(cols_first, cols_second, rows_first, rows_second, whi)
    middle = middle_of(lon)
    outer = [b for b in range(lon) if b not in middle]
    among = lambda ones, start: [(b * lat + i, b * lat + j) for b in ones for i, j in swap(lat, start)]
    axes = ("lon", "lat")
    rows_in_first = lax.ppermute(rows_first, axes, among(middle, 1) + among(outer, 0))
    rows_in_second = lax.ppermute(rows_second, axes, among(middle, 0) + among(outer, 1))

    mid, partial, s1, faces, edges = call(
        inner_kernel,
        [shape(5, 12, *slab), shape(n, 512), shape(4, 4, *slab), shape(5, 2, *slab), shape(18, *slab)],
        [VMEM] * 6,
        [
            pltpu.VMEM((4, LAT) + slab, F32),
            pltpu.VMEM((5, LAT) + slab, F32),
            pltpu.VMEM((10,) + slab, F32),
            pltpu.VMEM((2 * n, 12 * LON), BF16),
        ],
        size=8 << 20,
        flops=1 << 30,
    )(f, cols, cols_first, cols_second, whi, wlo)
    rim, values = call(
        rim_kernel,
        [shape(5, 4, *slab), shape(n, 512)],
        [VMEM] * 9,
        [pltpu.VMEM((2 * n, 4 * LON), BF16)],
        size=2 << 20,
        flops=1 << 28,
    )(f, edges, rows_in_first, rows_in_second, s1, faces, partial, whi, wlo)

    mirror = [(p * lon + b, (1 - p) * lon + lon - 1 - b) for p in range(2) for b in range(lon)]
    incoming = lax.ppermute(values, ("panel", "lon"), mirror)

    table, struck = call(
        table_kernel,
        [shape(512, LAT * LON, dtype=BF16), shape(8, LAT * LON)],
        [VMEM],
        size=2 << 20,
        flops=4 << 20,
    )(receivers)

    flow, warm = call(
        place_kernel,
        [shape(4, 1, DEP, LAT, LON), shape(1, DEP, LAT, LON)],
        [VMEM] * 5,
        [pltpu.VMEM((2 * n, 512), BF16), pltpu.VMEM((5, LAT) + slab, F32), pltpu.SemaphoreType.DMA((2, LAT))],
        out_specs=[ANY, ANY],
        size=8 << 20,
        flops=1 << 30,
    )(mid, rim, incoming, table, struck)
    return flow, warm


def solution(mesh):
    field = P("panel", None, "lat", "lon")
    tile = ("panel", "lat", "lon")
    in_specs = (
        P(None, "panel", None, "lat", "lon"),
        field,
        field,
        P(),
        P(*tile, None),
        P(*tile, None, None),
        P(*tile, None, None),
    )
    out_specs = (P(None, "panel", None, "lat", "lon"), field)
    return jax.shard_map(shards, mesh=mesh, in_specs=in_specs, out_specs=out_specs, check_vma=False)
```

```python
import jax
import jax.numpy as jnp
from jax import lax
from jax.experimental import pallas as pl
from jax.experimental.pallas import tpu as pltpu
from jax.sharding import PartitionSpec as P

OMEGA = 0.6
BETA = 0.5
TIME_STEP = 0.05
DIFFUSIVITY = 2.3

F32 = jnp.float32
BF16 = jnp.bfloat16
ANY = pl.BlockSpec(memory_space=pl.ANY)
VMEM = pl.BlockSpec(memory_space=pltpu.VMEM)
HBM = pl.BlockSpec(memory_space=pltpu.HBM)

LAT, DEP, LON = 16, 32, 128


def iota(dim, shape=(DEP, LON)):
    return lax.broadcasted_iota(jnp.int32, shape, dim)


def roll(x, shift, axis):
    return pltpu.roll(x, shift, axis)


def depth_pair(x):
    row = iota(0, x.shape)
    lower = jnp.where(row == 0, 0.0, roll(x, 1, 0))
    upper = jnp.where(row == x.shape[0] - 1, 0.0, roll(x, x.shape[0] - 1, 0))
    return lower, upper


def lon_pair(x, edge, r):
    return beside(x, roll(edge, 122 - 4 * r, 1))


def beside(x, halo):
    lane = iota(1, x.shape)
    lower = jnp.where(lane == 0, halo, roll(x, 1, 1))
    upper = jnp.where(lane == LON - 1, halo, roll(x, LON - 1, 1))
    return lower, upper


def swap_middle(c):
    pos = iota(1, c.shape) & 3
    return jnp.where(pos == 1, roll(c, LON - 1, 1), roll(c, 1, 1))


def sums(pairs, faces, eta, warmth):
    totals, change = [], 0.0
    for c in range(3):
        total = 4.0 * (warmth - 0.5) if c == 0 else 0.0
        for e in range(3):
            for face, value in zip(faces[e], pairs[c][e]):
                if value is not None:
                    total = total + face * value
        for sign, p, u in zip((-1, 1), pairs[3][c], pairs[c][c]):
            if p is not None:
                total = total - p if sign > 0 else total + p
                change = change - u if sign > 0 else change + u
        totals.append(total)
    return totals, (0.5 * BETA) * eta * change


def add_lat(totals, change, face, eta, values, upper):
    totals = [total + face * value for total, value in zip(totals, values)]
    part = (0.5 * BETA) * eta * values[1]
    if upper:
        return [totals[0], totals[1] - values[3], totals[2]], change - part
    return [totals[0], totals[1] + values[3], totals[2]], change + part


def settle(centre, totals, change, scale):
    return [(1.0 - OMEGA) * centre[c] + totals[c] * scale for c in range(3)] + [centre[3] + change]


def relax(centre, pairs, faces, scale, eta, warmth):
    return settle(centre, *sums(pairs, faces, eta, warmth), scale)


def odd(axis):
    return lax.rem(lax.axis_index(axis), 2) == 1


def middle_of(lon):
    return range(lon // 4, lon - lon // 4)


def first_above():
    b, middle = lax.axis_index("lon"), middle_of(lax.axis_size("lon"))
    return odd("lat") == jnp.logical_and(b >= middle.start, b < middle.stop)


def stage_kernel(
    motion, warmth, label, chart, receivers, donors, factors,
    f, cols_out, side_first_out, side_second_out, first_out, second_out, receivers_out, donors_out, factors_out,
    lab, table, sems,
):
    small = [
        pltpu.make_async_copy(chart, table, sems.at[3, 0]),
        pltpu.make_async_copy(receivers, receivers_out, sems.at[3, 1]),
        pltpu.make_async_copy(donors, donors_out, sems.at[3, 2]),
        pltpu.make_async_copy(factors, factors_out, sems.at[3, 3]),
    ]
    scalars, flow = [], []
    for r in range(LAT):
        scalars.append(pltpu.make_async_copy(warmth.at[0, :, r, :], f.at[5, r], sems.at[0, r]))
        scalars.append(pltpu.make_async_copy(label.at[0, :, r, :], lab.at[r], sems.at[1, r]))
        flow.append(pltpu.make_async_copy(motion.at[:, 0, :, r, :], f.at[0:4, r], sems.at[2, r]))
    for c in small[:1] + scalars + flow + small[1:]:
        c.start()
    small[0].wait()

    step = 4
    for start in range(0, LAT, step):
        for c in scalars[2 * start : 2 * (start + step)]:
            c.wait()
        for r in range(start, start + step):
            kind = lab[r]
            exponent = jnp.full(kind.shape, table[0], F32)
            for entry in range(1, 8):
                exponent = jnp.where(kind == entry, table[entry], exponent)
            f[4, r] = jnp.exp(exponent + DIFFUSIVITY * (0.5 - f[5, r]))

    group = iota(1) >> 2

    def pack(q, r, acc):
        first = roll(f[2 * q, r], 4 * r + 2, 1)
        second = roll(f[2 * q + 1, r], 4 * r + 66, 1)
        return jnp.where(group == r, first, jnp.where(group == r + 16, second, acc))

    packed = [jnp.zeros((DEP, LON), F32) for _ in range(3)]
    for start in range(0, LAT, step):
        rows = range(start, start + step)
        for r in rows:
            packed[2] = pack(2, r, packed[2])
        for c in flow[start : start + step]:
            c.wait()
        for r in rows:
            packed[0] = pack(0, r, packed[0])
            packed[1] = pack(1, r, packed[1])
    for q in range(3):
        cols_out[q] = packed[q]
    to_right, to_left = side_columns(packed, 0), side_columns(packed, 2)
    for i in range(2):
        rows = slice(0, DEP) if i == 0 else slice(DEP, DEP + DEP // 2)
        side_first_out[rows] = jnp.where(odd("lon"), to_right[i], to_left[i])
        side_second_out[rows] = jnp.where(odd("lon"), to_left[i], to_right[i])
    is_above = first_above()
    for out, above in ((first_out, is_above), (second_out, jnp.logical_not(is_above))):
        outer, inner = jnp.where(above, 14, 1), jnp.where(above, 15, 0)
        for k in range(5):
            out[block(k)] = f[k, outer]
        for k in range(6):
            out[block(5 + k)] = f[k, inner]
    for c in small[1:]:
        c.wait()


def block(i):
    return slice(i * DEP, (i + 1) * DEP)


def side_columns(packed, start):
    low_lanes = (iota(1) & 3) < 2
    low = [roll(p, (LON - start) % LON, 1) if start else p for p in packed]
    high = [roll(p, (2 - start) % LON, 1) if start != 2 else p for p in packed]
    half = DEP // 2
    return jnp.where(low_lanes, low[0], high[1]), jnp.where(low_lanes[:half], low[2][:half], high[2][half:])


def by_side(first, second):
    is_odd = odd("lon")
    return jnp.where(is_odd, second[...], first[...]), jnp.where(is_odd, first[...], second[...])


def from_sides(first, second):
    left_lanes = (iota(1) & 3) < 2
    left, right = by_side(first, second)
    l01, l2, r01, r2 = left[:DEP], left[DEP:], right[:DEP], right[DEP:]
    lefts = (l01, roll(l01, LON - 2, 1), jnp.concatenate([l2, roll(l2, LON - 2, 1)], axis=0))
    rights = (roll(r01, 2, 1), r01, jnp.concatenate([roll(r2, 2, 1), r2], axis=0))
    return [jnp.where(left_lanes, a, b) for a, b in zip(lefts, rights)]


CORNERS = slice(11 * DEP, 11 * DEP + 8)


def corners_kernel(cols_first, cols_second, rows_first, rows_second, _, first_out, second_out, c1, c2, sems):
    lane = iota(1, (8, LON))
    left_lanes, group = (lane & 3) < 2, (lane >> 2) & 15
    left, right = by_side(cols_first, cols_second)
    up = down = jnp.zeros((8, LON), F32)
    for j in range(4):
        for q in range(3):
            if q < 2:
                rows, from_left, from_right = slice(8 * j, 8 * j + 8), (0, -2)[q], (2, 0)[q]
            else:
                start = DEP + 8 * (j % 2)
                rows, from_left, from_right = slice(start, start + 8), (0, -2)[j // 2], (2, 0)[j // 2]
            move = 4 * q + 16 * j
            put = lambda x, shift: roll(x[rows], shift % LON, 1) if shift % LON else x[rows]
            to_up = jnp.where(left_lanes, put(left, from_left - move), put(right, from_right - move))
            to_down = jnp.where(left_lanes, put(left, from_left + move), put(right, from_right + move))
            up = jnp.where(group == 15 - q - 4 * j, to_up, up)
            down = jnp.where(group == q + 4 * j, to_down, down)
    c1[...] = jnp.where(first_above(), up, down)
    c2[...] = jnp.where(first_above(), down, up)
    a = pltpu.make_async_copy(c1, first_out.at[CORNERS], sems.at[0])
    b = pltpu.make_async_copy(c2, second_out.at[CORNERS], sems.at[1])
    a.start()
    b.start()
    a.wait()
    b.wait()


def weights_kernel(donors, factors, hi, lo):
    def body(i, _):
        cell = iota(0, (32, 512)) + i * 32
        w = jnp.zeros((32, 512), F32)
        for j in range(4):
            w = w + jnp.where(cell == donors[j : j + 1, :], factors[j : j + 1, :], 0.0)
        top = w.astype(BF16)
        at = pl.ds(pl.multiple_of(i * 32, 32), 32)
        hi[at, :] = top
        lo[at, :] = (w - top.astype(F32)).astype(BF16)
        return 0

    lax.fori_loop(0, LAT * LON // 32, body, 0)


def table_kernel(receivers, table, struck):
    columns = []
    for b in range(4):
        row = receivers[:, b * 128 : (b + 1) * 128].astype(F32)
        columns.append(jnp.broadcast_to(row, (128, 128)).T.astype(jnp.int32))

    def body(i, _):
        cell = iota(1, (128, LON)) + i * LON
        at = pl.ds(pl.multiple_of(i * LON, LON), LON)
        total = jnp.zeros((1, LON), F32)
        for b in range(4):
            hit = jnp.where(cell == columns[b], 1.0, 0.0)
            table[b * 128 : (b + 1) * 128, at] = hit.astype(BF16)
            total = total + jnp.sum(hit, axis=0, keepdims=True)
        struck[:, at] = jnp.broadcast_to(total, (8, LON))
        return 0

    lax.fori_loop(0, LAT, body, 0)


def edge_columns(cols, first, second):
    sides = from_sides(first, second)
    group = iota(1) >> 2
    here = jnp.logical_and(group >= 1, group <= LAT)
    halo, own = [], []
    for k in range(6):
        q, h = k // 2, k % 2
        halo.append(jnp.where(here, roll(sides[q], 4 + 64 * h, 1), 0.0))
        own.append(roll(cols[q], 4 + 64 * h, 1))
    return halo, own


def corner_columns(packed, k, up, lane):
    q, h = k // 2, k % 2
    parts = []
    for j in range(4):
        start = 64 * h + (60 - 4 * q - 16 * j if up else 4 * q + 16 * j)
        parts.append(roll(packed, (lane - start) % LON, 1))
    return jnp.concatenate(parts, axis=0)


def column_sums(halo, own):
    middle = (iota(1) & 3) == 1

    def pairs_of(k):
        c, o = halo[k], own[k]
        lower = jnp.where(middle, roll(c, 1, 1), roll(o, 1, 1))
        upper = jnp.where(middle, roll(o, LON - 1, 1), roll(c, LON - 1, 1))
        return depth_pair(c), (roll(c, 4, 1), roll(c, LON - 4, 1)), (lower, upper)

    faces = [[halo[4] + n for n in pair] for pair in pairs_of(4)]
    diagonal = faces[0][0] + faces[0][1] + faces[1][0] + faces[1][1] + faces[2][0] + faces[2][1]
    totals, change = sums([pairs_of(k) for k in range(4)], faces, halo[4], halo[5])
    return totals, change, diagonal


def columns_done(halo, totals, change, diagonal):
    inside = halo[4] > 0.0
    new = settle(halo[:4], totals, change, OMEGA / jnp.where(inside, diagonal, 1.0))
    return [jnp.where(inside, v, 0.0) for v in new]


def faces_of(eta, pairs):
    faces = [[eta + n for n in pair] for pair in pairs]
    diagonal = faces[0][0] + faces[0][1] + faces[1][0] + faces[1][1] + faces[2][0] + faces[2][1]
    return faces, OMEGA / jnp.where(diagonal > 0.0, diagonal, 1.0)


def advance(t, pairs, speed):
    change = 0.0
    for e, (lower, upper) in enumerate(pairs):
        change = (
            change
            - jnp.maximum(speed[e], 0.0) * (t - lower)
            - jnp.minimum(speed[e], 0.0) * (upper - t)
            + (upper + lower - 2.0 * t)
        )
    return t + TIME_STEP * change


def blend(lhs, hi, lo):
    n = 5 * DEP
    wide = jnp.dot(lhs, hi, preferred_element_type=F32)
    return wide[:n] + wide[n:] + jnp.dot(lhs[:n], lo, preferred_element_type=F32)


def put_split(lhs, k, at, value):
    top = value.astype(BF16)
    lhs[k * DEP : (k + 1) * DEP, at] = top
    lhs[(5 + k) * DEP : (6 + k) * DEP, at] = (value - top.astype(F32)).astype(BF16)


def inner_kernel(f, cols, cols_first, cols_second, whi, wlo, mid_out, values_out, s1_out, edges_out, parts_out, s1, faces, edge, lhs):
    halo, own = edge_columns(cols, cols_first, cols_second)
    for k in range(6):
        edge[k] = swap_middle(halo[k])
        edges_out[k], edges_out[6 + k] = halo[k], edge[k]
    totals, change, diagonal = column_sums(halo, own)
    for k, v in enumerate((*totals, change, diagonal)):
        edges_out[12 + k] = v
    for k, v in enumerate(columns_done(halo, totals, change, diagonal)):
        edge[6 + k] = swap_middle(v)

    def first(r, _):
        eta = f[4, r]
        both, scale = faces_of(eta, (depth_pair(eta), (f[4, r - 1], f[4, r + 1]), lon_pair(eta, edge[4], r)))
        for j, v in enumerate((both[0][0], both[0][1], both[2][0], both[2][1], scale)):
            faces[j, r] = v
        centre = [f[k, r] for k in range(4)]
        pairs = [(depth_pair(centre[k]), (f[k, r - 1], f[k, r + 1]), lon_pair(centre[k], edge[k], r)) for k in range(4)]
        for k, v in enumerate(relax(centre, pairs, both, scale, eta, f[5, r])):
            s1[k, r] = v
        return 0

    lax.fori_loop(1, LAT - 1, first, 0, unroll=7)

    def second(r):
        eta = f[4, r]
        both = ((faces[0, r], faces[1, r]), (eta + f[4, r - 1], eta + f[4, r + 1]), (faces[2, r], faces[3, r]))
        centre = [s1[k, r] for k in range(4)]
        pairs = [(depth_pair(centre[k]), (s1[k, r - 1], s1[k, r + 1]), lon_pair(centre[k], edge[6 + k], r)) for k in range(4)]
        t = f[5, r]
        new = relax(centre, pairs, both, faces[4, r], eta, t)
        new.append(advance(t, (depth_pair(t), (f[5, r - 1], f[5, r + 1]), lon_pair(t, edge[5], r)), new))
        at = slice((r - 2) * LON, (r - 1) * LON)
        for k in range(5):
            mid_out[k, r - 2] = new[k]
            put_split(lhs, k, at, new[k])

    total = jnp.zeros((5 * DEP, 512), F32)
    for start in range(2, LAT - 2, 2):
        second(start)
        second(start + 1)
        at, cells = slice((start - 2) * LON, start * LON), slice(start * LON, (start + 2) * LON)
        total = total + blend(lhs[:, at], whi[cells], wlo[cells])
    values_out[...] = total
    for j, r in enumerate((0, LAT - 1)):
        eta = f[4, r]
        lat = lambda k: (None if r == 0 else f[k, r - 1], None if r == LAT - 1 else f[k, r + 1])
        depth, lon = depth_pair(eta), lon_pair(eta, edge[4], r)
        inward = eta + f[4, 1 if r == 0 else r - 1]
        both = ([eta + n for n in depth], (inward, inward), [eta + n for n in lon])
        pairs = [(depth_pair(f[k, r]), lat(k), lon_pair(f[k, r], edge[k], r)) for k in range(4)]
        totals, change = sums(pairs, both, eta, f[5, r])
        diagonal = both[0][0] + both[0][1] + inward + both[2][0] + both[2][1]
        for i, v in enumerate((*totals, change, diagonal, *both[0], *both[2])):
            parts_out[j, i] = v
    for j, r in enumerate((1, LAT - 2)):
        eta = f[4, r]
        inward = eta + f[4, 2 if r == 1 else r - 1]
        lat = lambda k: (None, s1[k, 2]) if r == 1 else (s1[k, r - 1], None)
        both = ((faces[0, r], faces[1, r]), (inward, inward), (faces[2, r], faces[3, r]))
        pairs = [(depth_pair(s1[k, r]), lat(k), lon_pair(s1[k, r], edge[6 + k], r)) for k in range(4)]
        totals, change = sums(pairs, both, eta, f[5, r])
        for i, v in enumerate((*totals, change, faces[4, r])):
            parts_out[2 + j, i] = v
        for k in range(4):
            s1_out[k, j] = s1[k, r]


def rim_kernel(f, edges, rows_first, rows_second, s1_in, parts, partial, whi, wlo, rim_out, values_out, lhs):
    is_above = first_above()
    south = lambda at: jnp.where(is_above, rows_second[at], rows_first[at])
    north = lambda at: jnp.where(is_above, rows_first[at], rows_second[at])
    low, high = south(CORNERS), north(CORNERS)

    group = iota(1) >> 2
    halo = [edges[k] for k in range(6)]
    totals, change, diagonal = [edges[12 + c] for c in range(3)], edges[15], edges[16]
    for upper, packed, row in ((False, low, 0), (True, high, LAT - 1)):
        lanes = 4 * row + 4
        corner = [jnp.where(group == row + 1, corner_columns(packed, k, not upper, lanes), 0.0) for k in range(5)]
        diagonal = diagonal + corner[4]
        totals, change = add_lat(totals, change, halo[4] + corner[4], halo[4], corner[:4], upper)
    edge1 = [swap_middle(v) for v in columns_done(halo, totals, change, diagonal)]
    low_edge, high_edge = swap_middle(low), swap_middle(high)

    def edge(k, r):
        if r < 0:
            return corner_columns(low_edge, k, True, LON - 2)
        if r >= LAT:
            return corner_columns(high_edge, k, False, LON - 2)
        return roll(edges[6 + k], 122 - 4 * r, 1)

    def field(k, r):
        if r < 0:
            return south(block(k if r == -2 else 5 + k))
        if r >= LAT:
            return north(block(k if r == LAT + 1 else 5 + k))
        return f[k, r]

    s1, new = {}, {}
    for j, r in enumerate((1, LAT - 2)):
        s1[r] = [s1_in[k, j] for k in range(4)]
    for j, (out, r, inward) in enumerate(((-1, 0, 1), (LAT, LAT - 1, LAT - 2))):
        upper = out > r
        order = (lambda a, b: (b, a)) if upper else (lambda a, b: (a, b))
        eta = field(4, out)
        far = 2 * out - r
        both, scale = faces_of(eta, (depth_pair(eta), order(field(4, far), field(4, r)), beside(eta, edge(4, out))))
        centre = [field(k, out) for k in range(4)]
        pairs = [(depth_pair(centre[k]), order(field(k, far), field(k, r)), beside(centre[k], edge(k, out))) for k in range(4)]
        s1[out] = [jnp.where(eta > 0.0, v, 0.0) for v in relax(centre, pairs, both, scale, eta, field(5, out))]
        eta = f[4, r]
        outward = eta + field(4, out)
        scale = OMEGA / (parts[j, 4] + outward)
        totals, change = add_lat([parts[j, c] for c in range(3)], parts[j, 3], outward, eta, [field(k, out) for k in range(4)], upper)
        s1[r] = settle([f[k, r] for k in range(4)], totals, change, scale)
        inner_face = eta + f[4, inward]
        both = ((parts[j, 5], parts[j, 6]), order(outward, inner_face), (parts[j, 7], parts[j, 8]))
        pairs = [(depth_pair(s1[r][k]), order(s1[out][k], s1[inward][k]), lon_pair(s1[r][k], edge1[k], r)) for k in range(4)]
        new[r] = relax(s1[r], pairs, both, scale, eta, f[5, r])
        totals, change = add_lat([parts[2 + j, c] for c in range(3)], parts[2 + j, 3], inner_face, f[4, inward], s1[r], upper)
        new[inward] = settle(s1[inward], totals, change, parts[2 + j, 4])
    for j, r in enumerate((0, 1, LAT - 2, LAT - 1)):
        t = f[5, r]
        new[r].append(advance(t, (depth_pair(t), (field(5, r - 1), field(5, r + 1)), beside(t, edge(5, r))), new[r]))
        for k in range(5):
            rim_out[k, j] = new[r][k]
            put_split(lhs, k, slice(j * LON, (j + 1) * LON), new[r][k])
    low, high = slice(0, 2 * LON), slice(14 * LON, 16 * LON)
    values_out[...] = (
        partial[...] + blend(lhs[:, : 2 * LON], whi[low], wlo[low]) + blend(lhs[:, 2 * LON :], whi[high], wlo[high])
    )


def place_kernel(mid, rim, values, table, struck, flow_out, warmth_out, lhs, out, sems):
    n = 5 * DEP
    v = values[...]
    top = v.astype(BF16)
    lhs[0:n] = top
    lhs[n : 2 * n] = (v - top.astype(F32)).astype(BF16)
    copies = []
    half = LAT // 2
    for g in range(2):
        placed = jnp.dot(lhs[...], table[:, g * half * LON : (g + 1) * half * LON], preferred_element_type=F32)
        merged = placed[:n] + placed[n : 2 * n]
        for h in range(half):
            r = g * half + h
            hit = struck[0:1, r * LON : (r + 1) * LON] > 0.5
            for k in range(5):
                kept = mid[k, r - 2] if 2 <= r < 14 else rim[k, r if r < 2 else r - 12]
                out[k, r] = jnp.where(hit, merged[k * DEP : (k + 1) * DEP, h * LON : (h + 1) * LON], kept)
        for r in range(g * half, (g + 1) * half):
            copies.append(pltpu.make_async_copy(out.at[0:4, r], flow_out.at[:, 0, :, r, :], sems.at[0, r]))
            copies.append(pltpu.make_async_copy(out.at[4, r], warmth_out.at[0, :, r, :], sems.at[1, r]))
            copies[-2].start()
            copies[-1].start()
    for c in copies:
        c.wait()


def shape(*dims, dtype=F32):
    return jax.ShapeDtypeStruct(dims, dtype)


def call(kernel, outs, ins, scratch=(), out_specs=None, flops=0, size=0, aliases=None, limit=None):
    return pl.pallas_call(
        kernel,
        out_shape=outs,
        in_specs=ins,
        out_specs=out_specs or [VMEM] * len(outs),
        scratch_shapes=list(scratch),
        input_output_aliases=aliases or {},
        cost_estimate=pl.CostEstimate(flops=flops, bytes_accessed=size, transcendentals=0),
        compiler_params=pltpu.CompilerParams(vmem_limit_bytes=limit or (32 << 20)),
    )


def in_hbm(x):
    return pltpu.with_memory_space_constraint(x, pltpu.HBM)


def shards(motion, warmth, label, chart, receivers, donors, factors):
    lon, lat = lax.axis_size("lon"), lax.axis_size("lat")
    n, slab = 5 * DEP, (DEP, LON)

    sides, rows = shape(DEP + DEP // 2, LON), shape(11 * DEP + 8, LON)
    f, cols, side_first, side_second, rows_first, rows_second, receivers, donors, factors = call(
        stage_kernel,
        [
            shape(6, LAT, *slab), shape(3, *slab), sides, sides, rows, rows,
            shape(1, 512, dtype=jnp.int32), shape(4, 512, dtype=jnp.int32), shape(4, 512),
        ],
        [HBM] * 7,
        [pltpu.VMEM((LAT,) + slab, jnp.int32), pltpu.SMEM((8,), F32), pltpu.SemaphoreType.DMA((4, LAT))],
        size=2 << 20,
    )(*map(in_hbm, (motion, warmth, label, chart, receivers.reshape(1, 512), donors.reshape(4, 512), factors.reshape(4, 512))))

    swap = lambda n, start: [(i + j, i + 1 - j) for i in range(start, n - 1, 2) for j in range(2)]
    cols_first = lax.ppermute(side_first, "lon", swap(lon, 1))
    cols_second = lax.ppermute(side_second, "lon", swap(lon, 0))
    whi, wlo = call(
        weights_kernel,
        [shape(LAT * LON, 512, dtype=BF16), shape(LAT * LON, 512, dtype=BF16)],
        [VMEM, VMEM],
        size=4 << 20,
        flops=20 << 20,
    )(donors, factors)
    rows_first, rows_second = call(
        corners_kernel,
        [rows, rows],
        [VMEM, VMEM, ANY, ANY, ANY],
        [pltpu.VMEM((8, LON), F32), pltpu.VMEM((8, LON), F32), pltpu.SemaphoreType.DMA((2,))],
        out_specs=[ANY, ANY],
        aliases={2: 0, 3: 1},
        size=1 << 16,
    )(cols_first, cols_second, rows_first, rows_second, whi)
    middle = middle_of(lon)
    outer = [b for b in range(lon) if b not in middle]
    among = lambda ones, start: [(b * lat + i, b * lat + j) for b in ones for i, j in swap(lat, start)]
    axes = ("lon", "lat")
    rows_in_first = lax.ppermute(rows_first, axes, among(middle, 1) + among(outer, 0))
    rows_in_second = lax.ppermute(rows_second, axes, among(middle, 0) + among(outer, 1))

    mid, partial, s1, edges, parts = call(
        inner_kernel,
        [shape(5, 12, *slab), shape(n, 512), shape(4, 2, *slab), shape(17, *slab), shape(4, 9, *slab)],
        [VMEM] * 6,
        [
            pltpu.VMEM((4, LAT) + slab, F32),
            pltpu.VMEM((5, LAT) + slab, F32),
            pltpu.VMEM((10,) + slab, F32),
            pltpu.VMEM((2 * n, 12 * LON), BF16),
        ],
        size=8 << 20,
        flops=1 << 30,
    )(f, cols, cols_first, cols_second, whi, wlo)
    rim, values = call(
        rim_kernel,
        [shape(5, 4, *slab), shape(n, 512)],
        [VMEM] * 9,
        [pltpu.VMEM((2 * n, 4 * LON), BF16)],
        size=2 << 20,
        flops=1 << 28,
    )(f, edges, rows_in_first, rows_in_second, s1, parts, partial, whi, wlo)

    mirror = [(p * lon + b, (1 - p) * lon + lon - 1 - b) for p in range(2) for b in range(lon)]
    incoming = lax.ppermute(values, ("panel", "lon"), mirror)

    table, struck = call(
        table_kernel,
        [shape(512, LAT * LON, dtype=BF16), shape(8, LAT * LON)],
        [VMEM],
        size=2 << 20,
        flops=4 << 20,
    )(receivers)

    flow, warm = call(
        place_kernel,
        [shape(4, 1, DEP, LAT, LON), shape(1, DEP, LAT, LON)],
        [VMEM] * 5,
        [pltpu.VMEM((2 * n, 512), BF16), pltpu.VMEM((5, LAT) + slab, F32), pltpu.SemaphoreType.DMA((2, LAT))],
        out_specs=[ANY, ANY],
        size=8 << 20,
        flops=1 << 30,
    )(mid, rim, incoming, table, struck)
    return flow, warm


def solution(mesh):
    field = P("panel", None, "lat", "lon")
    tile = ("panel", "lat", "lon")
    in_specs = (
        P(None, "panel", None, "lat", "lon"),
        field,
        field,
        P(),
        P(*tile, None),
        P(*tile, None, None),
        P(*tile, None, None),
    )
    out_specs = (P(None, "panel", None, "lat", "lon"), field)
    return jax.shard_map(shards, mesh=mesh, in_specs=in_specs, out_specs=out_specs, check_vma=False)
```

```python
import jax
import jax.numpy as jnp
from jax import lax
from jax.experimental import pallas as pl
from jax.experimental.pallas import tpu as pltpu
from jax.sharding import PartitionSpec as P

OMEGA = 0.6
BETA = 0.5
TIME_STEP = 0.05
DIFFUSIVITY = 2.3

F32 = jnp.float32
BF16 = jnp.bfloat16
ANY = pl.BlockSpec(memory_space=pl.ANY)
VMEM = pl.BlockSpec(memory_space=pltpu.VMEM)
HBM = pl.BlockSpec(memory_space=pltpu.HBM)

LAT, DEP, LON = 16, 32, 128


def iota(dim, shape=(DEP, LON)):
    return lax.broadcasted_iota(jnp.int32, shape, dim)


def roll(x, shift, axis):
    return pltpu.roll(x, shift, axis)


def depth_pair(x):
    row = iota(0, x.shape)
    lower = jnp.where(row == 0, 0.0, roll(x, 1, 0))
    upper = jnp.where(row == x.shape[0] - 1, 0.0, roll(x, x.shape[0] - 1, 0))
    return lower, upper


def lon_pair(x, edge, r):
    return beside(x, roll(edge, 122 - 4 * r, 1))


def beside(x, halo):
    lane = iota(1, x.shape)
    lower = jnp.where(lane == 0, halo, roll(x, 1, 1))
    upper = jnp.where(lane == LON - 1, halo, roll(x, LON - 1, 1))
    return lower, upper


def swap_middle(c):
    pos = iota(1, c.shape) & 3
    return jnp.where(pos == 1, roll(c, LON - 1, 1), roll(c, 1, 1))


def sums(pairs, faces, eta, warmth):
    totals, change = [], 0.0
    for c in range(3):
        total = 4.0 * (warmth - 0.5) if c == 0 else 0.0
        for e in range(3):
            for face, value in zip(faces[e], pairs[c][e]):
                if value is not None:
                    total = total + face * value
        for sign, p, u in zip((-1, 1), pairs[3][c], pairs[c][c]):
            if p is not None:
                total = total - p if sign > 0 else total + p
                change = change - u if sign > 0 else change + u
        totals.append(total)
    return totals, (0.5 * BETA) * eta * change


def add_lat(totals, change, face, eta, values, upper):
    totals = [total + face * value for total, value in zip(totals, values)]
    part = (0.5 * BETA) * eta * values[1]
    if upper:
        return [totals[0], totals[1] - values[3], totals[2]], change - part
    return [totals[0], totals[1] + values[3], totals[2]], change + part


def settle(centre, totals, change, scale):
    return [(1.0 - OMEGA) * centre[c] + totals[c] * scale for c in range(3)] + [centre[3] + change]


def relax(centre, pairs, faces, scale, eta, warmth):
    return settle(centre, *sums(pairs, faces, eta, warmth), scale)


def odd(axis):
    return lax.rem(lax.axis_index(axis), 2) == 1


def middle_of(lon):
    return range(lon // 4, lon - lon // 4)


def first_above():
    b, middle = lax.axis_index("lon"), middle_of(lax.axis_size("lon"))
    return odd("lat") == jnp.logical_and(b >= middle.start, b < middle.stop)


def stage_kernel(
    motion, warmth, label, chart, receivers, donors, factors,
    f, cols_out, side_first_out, side_second_out, receivers_out, donors_out, factors_out,
    lab, table, sems,
):
    small = [
        pltpu.make_async_copy(chart, table, sems.at[3, 0]),
        pltpu.make_async_copy(receivers, receivers_out, sems.at[3, 1]),
        pltpu.make_async_copy(donors, donors_out, sems.at[3, 2]),
        pltpu.make_async_copy(factors, factors_out, sems.at[3, 3]),
    ]
    scalars, flow = [], []
    for r in range(LAT):
        scalars.append(pltpu.make_async_copy(warmth.at[0, :, r, :], f.at[5, r], sems.at[0, r]))
        scalars.append(pltpu.make_async_copy(label.at[0, :, r, :], lab.at[r], sems.at[1, r]))
        flow.append(pltpu.make_async_copy(motion.at[:, 0, :, r, :], f.at[0:4, r], sems.at[2, r]))
    for c in small[:1] + scalars + flow + small[1:]:
        c.start()
    small[0].wait()

    step = 4
    for start in range(0, LAT, step):
        for c in scalars[2 * start : 2 * (start + step)]:
            c.wait()
        for r in range(start, start + step):
            kind = lab[r]
            exponent = jnp.full(kind.shape, table[0], F32)
            for entry in range(1, 8):
                exponent = jnp.where(kind == entry, table[entry], exponent)
            f[4, r] = jnp.exp(exponent + DIFFUSIVITY * (0.5 - f[5, r]))

    group = iota(1) >> 2

    def pack(q, r, acc):
        first = roll(f[2 * q, r], 4 * r + 2, 1)
        second = roll(f[2 * q + 1, r], 4 * r + 66, 1)
        return jnp.where(group == r, first, jnp.where(group == r + 16, second, acc))

    packed = [jnp.zeros((DEP, LON), F32) for _ in range(3)]
    for start in range(0, LAT, step):
        rows = range(start, start + step)
        for r in rows:
            packed[2] = pack(2, r, packed[2])
        for c in flow[start : start + step]:
            c.wait()
        for r in rows:
            packed[0] = pack(0, r, packed[0])
            packed[1] = pack(1, r, packed[1])
    for q in range(3):
        cols_out[q] = packed[q]
    to_right, to_left = side_columns(packed, 0), side_columns(packed, 2)
    for i in range(2):
        rows = slice(0, DEP) if i == 0 else slice(DEP, DEP + DEP // 2)
        side_first_out[rows] = jnp.where(odd("lon"), to_right[i], to_left[i])
        side_second_out[rows] = jnp.where(odd("lon"), to_left[i], to_right[i])
    for c in small[1:]:
        c.wait()


def block(i):
    return slice(i * DEP, (i + 1) * DEP)


def side_columns(packed, start):
    low_lanes = (iota(1) & 3) < 2
    low = [roll(p, (LON - start) % LON, 1) if start else p for p in packed]
    high = [roll(p, (2 - start) % LON, 1) if start != 2 else p for p in packed]
    half = DEP // 2
    return jnp.where(low_lanes, low[0], high[1]), jnp.where(low_lanes[:half], low[2][:half], high[2][half:])


def by_side(first, second):
    is_odd = odd("lon")
    return jnp.where(is_odd, second[...], first[...]), jnp.where(is_odd, first[...], second[...])


def from_sides(first, second):
    left_lanes = (iota(1) & 3) < 2
    left, right = by_side(first, second)
    l01, l2, r01, r2 = left[:DEP], left[DEP:], right[:DEP], right[DEP:]
    lefts = (l01, roll(l01, LON - 2, 1), jnp.concatenate([l2, roll(l2, LON - 2, 1)], axis=0))
    rights = (roll(r01, 2, 1), r01, jnp.concatenate([roll(r2, 2, 1), r2], axis=0))
    return [jnp.where(left_lanes, a, b) for a, b in zip(lefts, rights)]


CORNERS = slice(11 * DEP, 11 * DEP + 8)


def corners_kernel(cols_first, cols_second, rows_first, rows_second, first_out, second_out, c1, c2, sems):
    lane = iota(1, (8, LON))
    left_lanes, group = (lane & 3) < 2, (lane >> 2) & 15
    left, right = by_side(cols_first, cols_second)
    up = down = jnp.zeros((8, LON), F32)
    for j in range(4):
        for q in range(3):
            if q < 2:
                rows, from_left, from_right = slice(8 * j, 8 * j + 8), (0, -2)[q], (2, 0)[q]
            else:
                start = DEP + 8 * (j % 2)
                rows, from_left, from_right = slice(start, start + 8), (0, -2)[j // 2], (2, 0)[j // 2]
            move = 4 * q + 16 * j
            put = lambda x, shift: roll(x[rows], shift % LON, 1) if shift % LON else x[rows]
            to_up = jnp.where(left_lanes, put(left, from_left - move), put(right, from_right - move))
            to_down = jnp.where(left_lanes, put(left, from_left + move), put(right, from_right + move))
            up = jnp.where(group == 15 - q - 4 * j, to_up, up)
            down = jnp.where(group == q + 4 * j, to_down, down)
    c1[...] = jnp.where(first_above(), up, down)
    c2[...] = jnp.where(first_above(), down, up)
    a = pltpu.make_async_copy(c1, first_out.at[CORNERS], sems.at[0])
    b = pltpu.make_async_copy(c2, second_out.at[CORNERS], sems.at[1])
    a.start()
    b.start()
    a.wait()
    b.wait()


def weights_kernel(donors, factors, f, hi, lo, first_out, second_out):
    is_above = first_above()
    for out, above in ((first_out, is_above), (second_out, jnp.logical_not(is_above))):
        outer, inner = jnp.where(above, 14, 1), jnp.where(above, 15, 0)
        for k in range(5):
            out[block(k)] = f[k, outer]
        for k in range(6):
            out[block(5 + k)] = f[k, inner]

    def body(i, _):
        cell = iota(0, (32, 512)) + i * 32
        w = jnp.zeros((32, 512), F32)
        for j in range(4):
            w = w + jnp.where(cell == donors[j : j + 1, :], factors[j : j + 1, :], 0.0)
        top = w.astype(BF16)
        at = pl.ds(pl.multiple_of(i * 32, 32), 32)
        hi[at, :] = top
        lo[at, :] = (w - top.astype(F32)).astype(BF16)
        return 0

    lax.fori_loop(0, LAT * LON // 32, body, 0)


def table_kernel(receivers, table, struck):
    columns = []
    for b in range(4):
        row = receivers[:, b * 128 : (b + 1) * 128].astype(F32)
        columns.append(jnp.broadcast_to(row, (128, 128)).T.astype(jnp.int32))

    def body(i, _):
        cell = iota(1, (128, LON)) + i * LON
        at = pl.ds(pl.multiple_of(i * LON, LON), LON)
        total = jnp.zeros((1, LON), F32)
        for b in range(4):
            hit = jnp.where(cell == columns[b], 1.0, 0.0)
            table[b * 128 : (b + 1) * 128, at] = hit.astype(BF16)
            total = total + jnp.sum(hit, axis=0, keepdims=True)
        struck[:, at] = jnp.broadcast_to(total, (8, LON))
        return 0

    lax.fori_loop(0, LAT, body, 0)


def edge_columns(cols, first, second):
    sides = from_sides(first, second)
    group = iota(1) >> 2
    here = jnp.logical_and(group >= 1, group <= LAT)
    halo, own = [], []
    for k in range(6):
        q, h = k // 2, k % 2
        halo.append(jnp.where(here, roll(sides[q], 4 + 64 * h, 1), 0.0))
        own.append(roll(cols[q], 4 + 64 * h, 1))
    return halo, own


def corner_columns(packed, k, up, lane):
    q, h = k // 2, k % 2
    parts = []
    for j in range(4):
        start = 64 * h + (60 - 4 * q - 16 * j if up else 4 * q + 16 * j)
        parts.append(roll(packed, (lane - start) % LON, 1))
    return jnp.concatenate(parts, axis=0)


def column_sums(halo, own):
    middle = (iota(1) & 3) == 1

    def pairs_of(k):
        c, o = halo[k], own[k]
        lower = jnp.where(middle, roll(c, 1, 1), roll(o, 1, 1))
        upper = jnp.where(middle, roll(o, LON - 1, 1), roll(c, LON - 1, 1))
        return depth_pair(c), (roll(c, 4, 1), roll(c, LON - 4, 1)), (lower, upper)

    faces = [[halo[4] + n for n in pair] for pair in pairs_of(4)]
    diagonal = faces[0][0] + faces[0][1] + faces[1][0] + faces[1][1] + faces[2][0] + faces[2][1]
    totals, change = sums([pairs_of(k) for k in range(4)], faces, halo[4], halo[5])
    return totals, change, diagonal


def columns_done(halo, totals, change, diagonal):
    inside = halo[4] > 0.0
    new = settle(halo[:4], totals, change, OMEGA / jnp.where(inside, diagonal, 1.0))
    return [jnp.where(inside, v, 0.0) for v in new]


def faces_of(eta, pairs):
    faces = [[eta + n for n in pair] for pair in pairs]
    diagonal = faces[0][0] + faces[0][1] + faces[1][0] + faces[1][1] + faces[2][0] + faces[2][1]
    return faces, OMEGA / jnp.where(diagonal > 0.0, diagonal, 1.0)


def advance(t, pairs, speed):
    change = 0.0
    for e, (lower, upper) in enumerate(pairs):
        change = (
            change
            - jnp.maximum(speed[e], 0.0) * (t - lower)
            - jnp.minimum(speed[e], 0.0) * (upper - t)
            + (upper + lower - 2.0 * t)
        )
    return t + TIME_STEP * change


def blend(lhs, hi, lo):
    n = 5 * DEP
    wide = jnp.dot(lhs, hi, preferred_element_type=F32)
    return wide[:n] + wide[n:] + jnp.dot(lhs[:n], lo, preferred_element_type=F32)


def put_split(lhs, k, at, value):
    top = value.astype(BF16)
    lhs[k * DEP : (k + 1) * DEP, at] = top
    lhs[(5 + k) * DEP : (6 + k) * DEP, at] = (value - top.astype(F32)).astype(BF16)


def inner_kernel(f, cols, cols_first, cols_second, whi, wlo, mid_out, values_out, s1_out, edges_out, parts_out, s1, faces, edge, lhs):
    halo, own = edge_columns(cols, cols_first, cols_second)
    for k in range(6):
        edge[k] = swap_middle(halo[k])
        edges_out[k], edges_out[6 + k] = halo[k], edge[k]
    totals, change, diagonal = column_sums(halo, own)
    for k, v in enumerate((*totals, change, diagonal)):
        edges_out[12 + k] = v
    for k, v in enumerate(columns_done(halo, totals, change, diagonal)):
        edge[6 + k] = swap_middle(v)

    def first(r, _):
        eta = f[4, r]
        both, scale = faces_of(eta, (depth_pair(eta), (f[4, r - 1], f[4, r + 1]), lon_pair(eta, edge[4], r)))
        for j, v in enumerate((both[0][0], both[0][1], both[2][0], both[2][1], scale)):
            faces[j, r] = v
        centre = [f[k, r] for k in range(4)]
        pairs = [(depth_pair(centre[k]), (f[k, r - 1], f[k, r + 1]), lon_pair(centre[k], edge[k], r)) for k in range(4)]
        for k, v in enumerate(relax(centre, pairs, both, scale, eta, f[5, r])):
            s1[k, r] = v
        return 0

    lax.fori_loop(1, LAT - 1, first, 0, unroll=7)

    def second(r):
        eta = f[4, r]
        both = ((faces[0, r], faces[1, r]), (eta + f[4, r - 1], eta + f[4, r + 1]), (faces[2, r], faces[3, r]))
        centre = [s1[k, r] for k in range(4)]
        pairs = [(depth_pair(centre[k]), (s1[k, r - 1], s1[k, r + 1]), lon_pair(centre[k], edge[6 + k], r)) for k in range(4)]
        t = f[5, r]
        new = relax(centre, pairs, both, faces[4, r], eta, t)
        new.append(advance(t, (depth_pair(t), (f[5, r - 1], f[5, r + 1]), lon_pair(t, edge[5], r)), new))
        at = slice((r - 2) * LON, (r - 1) * LON)
        for k in range(5):
            mid_out[k, r - 2] = new[k]
            put_split(lhs, k, at, new[k])

    total = jnp.zeros((5 * DEP, 512), F32)
    for start in range(2, LAT - 2, 2):
        second(start)
        second(start + 1)
        at, cells = slice((start - 2) * LON, start * LON), slice(start * LON, (start + 2) * LON)
        total = total + blend(lhs[:, at], whi[cells], wlo[cells])
    values_out[...] = total
    for j, r in enumerate((0, LAT - 1)):
        eta = f[4, r]
        lat = lambda k: (None if r == 0 else f[k, r - 1], None if r == LAT - 1 else f[k, r + 1])
        depth, lon = depth_pair(eta), lon_pair(eta, edge[4], r)
        inward = eta + f[4, 1 if r == 0 else r - 1]
        both = ([eta + n for n in depth], (inward, inward), [eta + n for n in lon])
        pairs = [(depth_pair(f[k, r]), lat(k), lon_pair(f[k, r], edge[k], r)) for k in range(4)]
        totals, change = sums(pairs, both, eta, f[5, r])
        diagonal = both[0][0] + both[0][1] + inward + both[2][0] + both[2][1]
        for i, v in enumerate((*totals, change, diagonal, *both[0], *both[2])):
            parts_out[j, i] = v
    for j, r in enumerate((1, LAT - 2)):
        eta = f[4, r]
        inward = eta + f[4, 2 if r == 1 else r - 1]
        lat = lambda k: (None, s1[k, 2]) if r == 1 else (s1[k, r - 1], None)
        both = ((faces[0, r], faces[1, r]), (inward, inward), (faces[2, r], faces[3, r]))
        pairs = [(depth_pair(s1[k, r]), lat(k), lon_pair(s1[k, r], edge[6 + k], r)) for k in range(4)]
        totals, change = sums(pairs, both, eta, f[5, r])
        for i, v in enumerate((*totals, change, faces[4, r])):
            parts_out[2 + j, i] = v
        for k in range(4):
            s1_out[k, j] = s1[k, r]


def rim_kernel(f, edges, rows_first, rows_second, s1_in, parts, partial, whi, wlo, rim_out, values_out, lhs):
    is_above = first_above()
    south = lambda at: jnp.where(is_above, rows_second[at], rows_first[at])
    north = lambda at: jnp.where(is_above, rows_first[at], rows_second[at])
    low, high = south(CORNERS), north(CORNERS)

    group = iota(1) >> 2
    halo = [edges[k] for k in range(6)]
    totals, change, diagonal = [edges[12 + c] for c in range(3)], edges[15], edges[16]
    for upper, packed, row in ((False, low, 0), (True, high, LAT - 1)):
        lanes = 4 * row + 4
        corner = [jnp.where(group == row + 1, corner_columns(packed, k, not upper, lanes), 0.0) for k in range(5)]
        diagonal = diagonal + corner[4]
        totals, change = add_lat(totals, change, halo[4] + corner[4], halo[4], corner[:4], upper)
    edge1 = [swap_middle(v) for v in columns_done(halo, totals, change, diagonal)]
    low_edge, high_edge = swap_middle(low), swap_middle(high)

    def edge(k, r):
        if r < 0:
            return corner_columns(low_edge, k, True, LON - 2)
        if r >= LAT:
            return corner_columns(high_edge, k, False, LON - 2)
        return roll(edges[6 + k], 122 - 4 * r, 1)

    def field(k, r):
        if r < 0:
            return south(block(k if r == -2 else 5 + k))
        if r >= LAT:
            return north(block(k if r == LAT + 1 else 5 + k))
        return f[k, r]

    s1, new = {}, {}
    for j, r in enumerate((1, LAT - 2)):
        s1[r] = [s1_in[k, j] for k in range(4)]
    for j, (out, r, inward) in enumerate(((-1, 0, 1), (LAT, LAT - 1, LAT - 2))):
        upper = out > r
        order = (lambda a, b: (b, a)) if upper else (lambda a, b: (a, b))
        eta = field(4, out)
        far = 2 * out - r
        both, scale = faces_of(eta, (depth_pair(eta), order(field(4, far), field(4, r)), beside(eta, edge(4, out))))
        centre = [field(k, out) for k in range(4)]
        pairs = [(depth_pair(centre[k]), order(field(k, far), field(k, r)), beside(centre[k], edge(k, out))) for k in range(4)]
        s1[out] = [jnp.where(eta > 0.0, v, 0.0) for v in relax(centre, pairs, both, scale, eta, field(5, out))]
        eta = f[4, r]
        outward = eta + field(4, out)
        scale = OMEGA / (parts[j, 4] + outward)
        totals, change = add_lat([parts[j, c] for c in range(3)], parts[j, 3], outward, eta, [field(k, out) for k in range(4)], upper)
        s1[r] = settle([f[k, r] for k in range(4)], totals, change, scale)
        inner_face = eta + f[4, inward]
        both = ((parts[j, 5], parts[j, 6]), order(outward, inner_face), (parts[j, 7], parts[j, 8]))
        pairs = [(depth_pair(s1[r][k]), order(s1[out][k], s1[inward][k]), lon_pair(s1[r][k], edge1[k], r)) for k in range(4)]
        new[r] = relax(s1[r], pairs, both, scale, eta, f[5, r])
        totals, change = add_lat([parts[2 + j, c] for c in range(3)], parts[2 + j, 3], inner_face, f[4, inward], s1[r], upper)
        new[inward] = settle(s1[inward], totals, change, parts[2 + j, 4])
    for j, r in enumerate((0, 1, LAT - 2, LAT - 1)):
        t = f[5, r]
        new[r].append(advance(t, (depth_pair(t), (field(5, r - 1), field(5, r + 1)), beside(t, edge(5, r))), new[r]))
        for k in range(5):
            rim_out[k, j] = new[r][k]
            put_split(lhs, k, slice(j * LON, (j + 1) * LON), new[r][k])
    low, high = slice(0, 2 * LON), slice(14 * LON, 16 * LON)
    values_out[...] = (
        partial[...] + blend(lhs[:, : 2 * LON], whi[low], wlo[low]) + blend(lhs[:, 2 * LON :], whi[high], wlo[high])
    )


def place_kernel(mid, rim, values, table, struck, flow_out, warmth_out, lhs, out, sems):
    n = 5 * DEP
    v = values[...]
    top = v.astype(BF16)
    lhs[0:n] = top
    lhs[n : 2 * n] = (v - top.astype(F32)).astype(BF16)
    copies = []
    half = LAT // 2
    for g in range(2):
        placed = jnp.dot(lhs[...], table[:, g * half * LON : (g + 1) * half * LON], preferred_element_type=F32)
        merged = placed[:n] + placed[n : 2 * n]
        for h in range(half):
            r = g * half + h
            hit = struck[0:1, r * LON : (r + 1) * LON] > 0.5
            for k in range(5):
                kept = mid[k, r - 2] if 2 <= r < 14 else rim[k, r if r < 2 else r - 12]
                out[k, r] = jnp.where(hit, merged[k * DEP : (k + 1) * DEP, h * LON : (h + 1) * LON], kept)
        for r in range(g * half, (g + 1) * half):
            copies.append(pltpu.make_async_copy(out.at[0:4, r], flow_out.at[:, 0, :, r, :], sems.at[0, r]))
            copies.append(pltpu.make_async_copy(out.at[4, r], warmth_out.at[0, :, r, :], sems.at[1, r]))
            copies[-2].start()
            copies[-1].start()
    for c in copies:
        c.wait()


def shape(*dims, dtype=F32):
    return jax.ShapeDtypeStruct(dims, dtype)


def call(kernel, outs, ins, scratch=(), out_specs=None, flops=0, size=0, aliases=None, limit=None):
    return pl.pallas_call(
        kernel,
        out_shape=outs,
        in_specs=ins,
        out_specs=out_specs or [VMEM] * len(outs),
        scratch_shapes=list(scratch),
        input_output_aliases=aliases or {},
        cost_estimate=pl.CostEstimate(flops=flops, bytes_accessed=size, transcendentals=0),
        compiler_params=pltpu.CompilerParams(vmem_limit_bytes=limit or (32 << 20)),
    )


def in_hbm(x):
    return pltpu.with_memory_space_constraint(x, pltpu.HBM)


def shards(motion, warmth, label, chart, receivers, donors, factors):
    lon, lat = lax.axis_size("lon"), lax.axis_size("lat")
    n, slab = 5 * DEP, (DEP, LON)

    sides, rows = shape(DEP + DEP // 2, LON), shape(11 * DEP + 8, LON)
    f, cols, side_first, side_second, receivers, donors, factors = call(
        stage_kernel,
        [
            shape(6, LAT, *slab), shape(3, *slab), sides, sides,
            shape(1, 512, dtype=jnp.int32), shape(4, 512, dtype=jnp.int32), shape(4, 512),
        ],
        [HBM] * 7,
        [pltpu.VMEM((LAT,) + slab, jnp.int32), pltpu.SMEM((8,), F32), pltpu.SemaphoreType.DMA((4, LAT))],
        size=2 << 20,
    )(*map(in_hbm, (motion, warmth, label, chart, receivers.reshape(1, 512), donors.reshape(4, 512), factors.reshape(4, 512))))

    swap = lambda n, start: [(i + j, i + 1 - j) for i in range(start, n - 1, 2) for j in range(2)]
    cols_first = lax.ppermute(side_first, "lon", swap(lon, 1))
    cols_second = lax.ppermute(side_second, "lon", swap(lon, 0))
    whi, wlo, rows_first, rows_second = call(
        weights_kernel,
        [shape(LAT * LON, 512, dtype=BF16), shape(LAT * LON, 512, dtype=BF16), rows, rows],
        [VMEM, VMEM, VMEM],
        size=4 << 20,
        flops=20 << 20,
    )(donors, factors, f)
    rows_first, rows_second = call(
        corners_kernel,
        [rows, rows],
        [VMEM, VMEM, ANY, ANY],
        [pltpu.VMEM((8, LON), F32), pltpu.VMEM((8, LON), F32), pltpu.SemaphoreType.DMA((2,))],
        out_specs=[ANY, ANY],
        aliases={2: 0, 3: 1},
        size=1 << 16,
    )(cols_first, cols_second, rows_first, rows_second)
    middle = middle_of(lon)
    outer = [b for b in range(lon) if b not in middle]
    among = lambda ones, start: [(b * lat + i, b * lat + j) for b in ones for i, j in swap(lat, start)]
    axes = ("lon", "lat")
    rows_in_first = lax.ppermute(rows_first, axes, among(middle, 1) + among(outer, 0))
    rows_in_second = lax.ppermute(rows_second, axes, among(middle, 0) + among(outer, 1))

    mid, partial, s1, edges, parts = call(
        inner_kernel,
        [shape(5, 12, *slab), shape(n, 512), shape(4, 2, *slab), shape(17, *slab), shape(4, 9, *slab)],
        [VMEM] * 6,
        [
            pltpu.VMEM((4, LAT) + slab, F32),
            pltpu.VMEM((5, LAT) + slab, F32),
            pltpu.VMEM((10,) + slab, F32),
            pltpu.VMEM((2 * n, 12 * LON), BF16),
        ],
        size=8 << 20,
        flops=1 << 30,
    )(f, cols, cols_first, cols_second, whi, wlo)
    rim, values = call(
        rim_kernel,
        [shape(5, 4, *slab), shape(n, 512)],
        [VMEM] * 9,
        [pltpu.VMEM((2 * n, 4 * LON), BF16)],
        size=2 << 20,
        flops=1 << 28,
    )(f, edges, rows_in_first, rows_in_second, s1, parts, partial, whi, wlo)

    mirror = [(p * lon + b, (1 - p) * lon + lon - 1 - b) for p in range(2) for b in range(lon)]
    incoming = lax.ppermute(values, ("panel", "lon"), mirror)

    table, struck = call(
        table_kernel,
        [shape(512, LAT * LON, dtype=BF16), shape(8, LAT * LON)],
        [VMEM],
        size=2 << 20,
        flops=4 << 20,
    )(receivers)

    flow, warm = call(
        place_kernel,
        [shape(4, 1, DEP, LAT, LON), shape(1, DEP, LAT, LON)],
        [VMEM] * 5,
        [pltpu.VMEM((2 * n, 512), BF16), pltpu.VMEM((5, LAT) + slab, F32), pltpu.SemaphoreType.DMA((2, LAT))],
        out_specs=[ANY, ANY],
        size=8 << 20,
        flops=1 << 30,
    )(mid, rim, incoming, table, struck)
    return flow, warm


def solution(mesh):
    field = P("panel", None, "lat", "lon")
    tile = ("panel", "lat", "lon")
    in_specs = (
        P(None, "panel", None, "lat", "lon"),
        field,
        field,
        P(),
        P(*tile, None),
        P(*tile, None, None),
        P(*tile, None, None),
    )
    out_specs = (P(None, "panel", None, "lat", "lon"), field)
    return jax.shard_map(shards, mesh=mesh, in_specs=in_specs, out_specs=out_specs, check_vma=False)
```

```python
import jax
import jax.numpy as jnp
from jax import lax
from jax.experimental import pallas as pl
from jax.experimental.pallas import tpu as pltpu
from jax.sharding import PartitionSpec as P

OMEGA = 0.6
BETA = 0.5
TIME_STEP = 0.05
DIFFUSIVITY = 2.3

F32 = jnp.float32
BF16 = jnp.bfloat16
ANY = pl.BlockSpec(memory_space=pl.ANY)
VMEM = pl.BlockSpec(memory_space=pltpu.VMEM)
HBM = pl.BlockSpec(memory_space=pltpu.HBM)

LAT, DEP, LON = 16, 32, 128


def iota(dim, shape=(DEP, LON)):
    return lax.broadcasted_iota(jnp.int32, shape, dim)


def roll(x, shift, axis):
    return pltpu.roll(x, shift, axis)


def depth_pair(x):
    row = iota(0, x.shape)
    lower = jnp.where(row == 0, 0.0, roll(x, 1, 0))
    upper = jnp.where(row == x.shape[0] - 1, 0.0, roll(x, x.shape[0] - 1, 0))
    return lower, upper


def lon_pair(x, edge, r):
    return beside(x, roll(edge, 122 - 4 * r, 1))


def beside(x, halo):
    lane = iota(1, x.shape)
    lower = jnp.where(lane == 0, halo, roll(x, 1, 1))
    upper = jnp.where(lane == LON - 1, halo, roll(x, LON - 1, 1))
    return lower, upper


def swap_middle(c):
    pos = iota(1, c.shape) & 3
    return jnp.where(pos == 1, roll(c, LON - 1, 1), roll(c, 1, 1))


def sums(pairs, faces, eta, warmth):
    totals, change = [], 0.0
    for c in range(3):
        total = 4.0 * (warmth - 0.5) if c == 0 else 0.0
        for e in range(3):
            for face, value in zip(faces[e], pairs[c][e]):
                if value is not None:
                    total = total + face * value
        for sign, p, u in zip((-1, 1), pairs[3][c], pairs[c][c]):
            if p is not None:
                total = total - p if sign > 0 else total + p
                change = change - u if sign > 0 else change + u
        totals.append(total)
    return totals, (0.5 * BETA) * eta * change


def add_lat(totals, change, face, eta, values, upper):
    totals = [total + face * value for total, value in zip(totals, values)]
    part = (0.5 * BETA) * eta * values[1]
    if upper:
        return [totals[0], totals[1] - values[3], totals[2]], change - part
    return [totals[0], totals[1] + values[3], totals[2]], change + part


def settle(centre, totals, change, scale):
    return [(1.0 - OMEGA) * centre[c] + totals[c] * scale for c in range(3)] + [centre[3] + change]


def relax(centre, pairs, faces, scale, eta, warmth):
    return settle(centre, *sums(pairs, faces, eta, warmth), scale)


def odd(axis):
    return lax.rem(lax.axis_index(axis), 2) == 1


def middle_of(lon):
    return range(lon // 4, lon - lon // 4)


def first_above():
    b, middle = lax.axis_index("lon"), middle_of(lax.axis_size("lon"))
    return odd("lat") == jnp.logical_and(b >= middle.start, b < middle.stop)


def stage_kernel(
    motion, warmth, label, chart, receivers, donors, factors,
    f, cols_out, side_first_out, side_second_out, first_out, second_out, receivers_out, donors_out, factors_out,
    lab, table, sems,
):
    small = [
        pltpu.make_async_copy(chart, table, sems.at[3, 0]),
        pltpu.make_async_copy(receivers, receivers_out, sems.at[3, 1]),
        pltpu.make_async_copy(donors, donors_out, sems.at[3, 2]),
        pltpu.make_async_copy(factors, factors_out, sems.at[3, 3]),
    ]
    scalars, flow = [], []
    for r in range(LAT):
        scalars.append(pltpu.make_async_copy(warmth.at[0, :, r, :], f.at[5, r], sems.at[0, r]))
        scalars.append(pltpu.make_async_copy(label.at[0, :, r, :], lab.at[r], sems.at[1, r]))
        flow.append(pltpu.make_async_copy(motion.at[:, 0, :, r, :], f.at[0:4, r], sems.at[2, r]))
    for c in small[:1] + scalars + flow + small[1:]:
        c.start()
    small[0].wait()

    step = 2
    for start in range(0, LAT, step):
        for c in scalars[2 * start : 2 * (start + step)]:
            c.wait()
        for r in range(start, start + step):
            kind = lab[r]
            exponent = jnp.full(kind.shape, table[0], F32)
            for entry in range(1, 8):
                exponent = jnp.where(kind == entry, table[entry], exponent)
            f[4, r] = jnp.exp(exponent + DIFFUSIVITY * (0.5 - f[5, r]))

    group = iota(1) >> 2

    def pack(q, r, acc):
        first = roll(f[2 * q, r], 4 * r + 2, 1)
        second = roll(f[2 * q + 1, r], 4 * r + 66, 1)
        return jnp.where(group == r, first, jnp.where(group == r + 16, second, acc))

    packed = [jnp.zeros((DEP, LON), F32) for _ in range(3)]
    for start in range(0, LAT, step):
        rows = range(start, start + step)
        for r in rows:
            packed[2] = pack(2, r, packed[2])
        for c in flow[start : start + step]:
            c.wait()
        for r in rows:
            packed[0] = pack(0, r, packed[0])
            packed[1] = pack(1, r, packed[1])
    for q in range(3):
        cols_out[q] = packed[q]
    to_right, to_left = side_columns(packed, 0), side_columns(packed, 2)
    for i in range(2):
        rows = slice(0, DEP) if i == 0 else slice(DEP, DEP + DEP // 2)
        side_first_out[rows] = jnp.where(odd("lon"), to_right[i], to_left[i])
        side_second_out[rows] = jnp.where(odd("lon"), to_left[i], to_right[i])
    is_above = first_above()
    for out, above in ((first_out, is_above), (second_out, jnp.logical_not(is_above))):
        outer, inner = jnp.where(above, 14, 1), jnp.where(above, 15, 0)
        for k in range(5):
            out[block(k)] = f[k, outer]
        for k in range(6):
            out[block(5 + k)] = f[k, inner]
    for c in small[1:]:
        c.wait()


def block(i):
    return slice(i * DEP, (i + 1) * DEP)


def side_columns(packed, start):
    low_lanes = (iota(1) & 3) < 2
    low = [roll(p, (LON - start) % LON, 1) if start else p for p in packed]
    high = [roll(p, (2 - start) % LON, 1) if start != 2 else p for p in packed]
    half = DEP // 2
    return jnp.where(low_lanes, low[0], high[1]), jnp.where(low_lanes[:half], low[2][:half], high[2][half:])


def by_side(first, second):
    is_odd = odd("lon")
    return jnp.where(is_odd, second[...], first[...]), jnp.where(is_odd, first[...], second[...])


def from_sides(first, second):
    left_lanes = (iota(1) & 3) < 2
    left, right = by_side(first, second)
    l01, l2, r01, r2 = left[:DEP], left[DEP:], right[:DEP], right[DEP:]
    lefts = (l01, roll(l01, LON - 2, 1), jnp.concatenate([l2, roll(l2, LON - 2, 1)], axis=0))
    rights = (roll(r01, 2, 1), r01, jnp.concatenate([roll(r2, 2, 1), r2], axis=0))
    return [jnp.where(left_lanes, a, b) for a, b in zip(lefts, rights)]


CORNERS = slice(11 * DEP, 11 * DEP + 8)


def corners_kernel(cols_first, cols_second, rows_first, rows_second, _, first_out, second_out, c1, c2, sems):
    lane = iota(1, (8, LON))
    left_lanes, group = (lane & 3) < 2, (lane >> 2) & 15
    left, right = by_side(cols_first, cols_second)
    up = down = jnp.zeros((8, LON), F32)
    for j in range(4):
        for q in range(3):
            if q < 2:
                rows, from_left, from_right = slice(8 * j, 8 * j + 8), (0, -2)[q], (2, 0)[q]
            else:
                start = DEP + 8 * (j % 2)
                rows, from_left, from_right = slice(start, start + 8), (0, -2)[j // 2], (2, 0)[j // 2]
            move = 4 * q + 16 * j
            put = lambda x, shift: roll(x[rows], shift % LON, 1) if shift % LON else x[rows]
            to_up = jnp.where(left_lanes, put(left, from_left - move), put(right, from_right - move))
            to_down = jnp.where(left_lanes, put(left, from_left + move), put(right, from_right + move))
            up = jnp.where(group == 15 - q - 4 * j, to_up, up)
            down = jnp.where(group == q + 4 * j, to_down, down)
    c1[...] = jnp.where(first_above(), up, down)
    c2[...] = jnp.where(first_above(), down, up)
    a = pltpu.make_async_copy(c1, first_out.at[CORNERS], sems.at[0])
    b = pltpu.make_async_copy(c2, second_out.at[CORNERS], sems.at[1])
    a.start()
    b.start()
    a.wait()
    b.wait()


def weights_kernel(donors, factors, hi, lo):
    def body(i, _):
        cell = iota(0, (32, 512)) + i * 32
        w = jnp.zeros((32, 512), F32)
        for j in range(4):
            w = w + jnp.where(cell == donors[j : j + 1, :], factors[j : j + 1, :], 0.0)
        top = w.astype(BF16)
        at = pl.ds(pl.multiple_of(i * 32, 32), 32)
        hi[at, :] = top
        lo[at, :] = (w - top.astype(F32)).astype(BF16)
        return 0

    lax.fori_loop(0, LAT * LON // 32, body, 0)


def table_kernel(receivers, table, struck):
    columns = []
    for b in range(4):
        row = receivers[:, b * 128 : (b + 1) * 128].astype(F32)
        columns.append(jnp.broadcast_to(row, (128, 128)).T.astype(jnp.int32))

    def body(i, _):
        cell = iota(1, (128, LON)) + i * LON
        at = pl.ds(pl.multiple_of(i * LON, LON), LON)
        total = jnp.zeros((1, LON), F32)
        for b in range(4):
            hit = jnp.where(cell == columns[b], 1.0, 0.0)
            table[b * 128 : (b + 1) * 128, at] = hit.astype(BF16)
            total = total + jnp.sum(hit, axis=0, keepdims=True)
        struck[:, at] = jnp.broadcast_to(total, (8, LON))
        return 0

    lax.fori_loop(0, LAT, body, 0)


def edge_columns(cols, first, second):
    sides = from_sides(first, second)
    group = iota(1) >> 2
    here = jnp.logical_and(group >= 1, group <= LAT)
    halo, own = [], []
    for k in range(6):
        q, h = k // 2, k % 2
        halo.append(jnp.where(here, roll(sides[q], 4 + 64 * h, 1), 0.0))
        own.append(roll(cols[q], 4 + 64 * h, 1))
    return halo, own


def corner_columns(packed, k, up, lane):
    q, h = k // 2, k % 2
    parts = []
    for j in range(4):
        start = 64 * h + (60 - 4 * q - 16 * j if up else 4 * q + 16 * j)
        parts.append(roll(packed, (lane - start) % LON, 1))
    return jnp.concatenate(parts, axis=0)


def column_sums(halo, own):
    middle = (iota(1) & 3) == 1

    def pairs_of(k):
        c, o = halo[k], own[k]
        lower = jnp.where(middle, roll(c, 1, 1), roll(o, 1, 1))
        upper = jnp.where(middle, roll(o, LON - 1, 1), roll(c, LON - 1, 1))
        return depth_pair(c), (roll(c, 4, 1), roll(c, LON - 4, 1)), (lower, upper)

    faces = [[halo[4] + n for n in pair] for pair in pairs_of(4)]
    diagonal = faces[0][0] + faces[0][1] + faces[1][0] + faces[1][1] + faces[2][0] + faces[2][1]
    totals, change = sums([pairs_of(k) for k in range(4)], faces, halo[4], halo[5])
    return totals, change, diagonal


def columns_done(halo, totals, change, diagonal):
    inside = halo[4] > 0.0
    new = settle(halo[:4], totals, change, OMEGA / jnp.where(inside, diagonal, 1.0))
    return [jnp.where(inside, v, 0.0) for v in new]


def faces_of(eta, pairs):
    faces = [[eta + n for n in pair] for pair in pairs]
    diagonal = faces[0][0] + faces[0][1] + faces[1][0] + faces[1][1] + faces[2][0] + faces[2][1]
    return faces, OMEGA / jnp.where(diagonal > 0.0, diagonal, 1.0)


def advance(t, pairs, speed):
    change = 0.0
    for e, (lower, upper) in enumerate(pairs):
        change = (
            change
            - jnp.maximum(speed[e], 0.0) * (t - lower)
            - jnp.minimum(speed[e], 0.0) * (upper - t)
            + (upper + lower - 2.0 * t)
        )
    return t + TIME_STEP * change


def blend(lhs, hi, lo):
    n = 5 * DEP
    wide = jnp.dot(lhs, hi, preferred_element_type=F32)
    return wide[:n] + wide[n:] + jnp.dot(lhs[:n], lo, preferred_element_type=F32)


def put_split(lhs, k, at, value):
    top = value.astype(BF16)
    lhs[k * DEP : (k + 1) * DEP, at] = top
    lhs[(5 + k) * DEP : (6 + k) * DEP, at] = (value - top.astype(F32)).astype(BF16)


def inner_kernel(f, cols, cols_first, cols_second, whi, wlo, mid_out, values_out, s1_out, edges_out, parts_out, s1, faces, edge, lhs):
    halo, own = edge_columns(cols, cols_first, cols_second)
    for k in range(6):
        edge[k] = swap_middle(halo[k])
        edges_out[k], edges_out[6 + k] = halo[k], edge[k]
    totals, change, diagonal = column_sums(halo, own)
    for k, v in enumerate((*totals, change, diagonal)):
        edges_out[12 + k] = v
    for k, v in enumerate(columns_done(halo, totals, change, diagonal)):
        edge[6 + k] = swap_middle(v)

    def first(r, _):
        eta = f[4, r]
        both, scale = faces_of(eta, (depth_pair(eta), (f[4, r - 1], f[4, r + 1]), lon_pair(eta, edge[4], r)))
        for j, v in enumerate((both[0][0], both[0][1], both[2][0], both[2][1], scale)):
            faces[j, r] = v
        centre = [f[k, r] for k in range(4)]
        pairs = [(depth_pair(centre[k]), (f[k, r - 1], f[k, r + 1]), lon_pair(centre[k], edge[k], r)) for k in range(4)]
        for k, v in enumerate(relax(centre, pairs, both, scale, eta, f[5, r])):
            s1[k, r] = v
        return 0

    lax.fori_loop(1, LAT - 1, first, 0, unroll=7)

    def second(r):
        eta = f[4, r]
        both = ((faces[0, r], faces[1, r]), (eta + f[4, r - 1], eta + f[4, r + 1]), (faces[2, r], faces[3, r]))
        centre = [s1[k, r] for k in range(4)]
        pairs = [(depth_pair(centre[k]), (s1[k, r - 1], s1[k, r + 1]), lon_pair(centre[k], edge[6 + k], r)) for k in range(4)]
        t = f[5, r]
        new = relax(centre, pairs, both, faces[4, r], eta, t)
        new.append(advance(t, (depth_pair(t), (f[5, r - 1], f[5, r + 1]), lon_pair(t, edge[5], r)), new))
        at = slice((r - 2) * LON, (r - 1) * LON)
        for k in range(5):
            mid_out[k, r - 2] = new[k]
            put_split(lhs, k, at, new[k])

    total = jnp.zeros((5 * DEP, 512), F32)
    for start in range(2, LAT - 2, 2):
        second(start)
        second(start + 1)
        at, cells = slice((start - 2) * LON, start * LON), slice(start * LON, (start + 2) * LON)
        total = total + blend(lhs[:, at], whi[cells], wlo[cells])
    values_out[...] = total
    for j, r in enumerate((0, LAT - 1)):
        eta = f[4, r]
        lat = lambda k: (None if r == 0 else f[k, r - 1], None if r == LAT - 1 else f[k, r + 1])
        depth, lon = depth_pair(eta), lon_pair(eta, edge[4], r)
        inward = eta + f[4, 1 if r == 0 else r - 1]
        both = ([eta + n for n in depth], (inward, inward), [eta + n for n in lon])
        pairs = [(depth_pair(f[k, r]), lat(k), lon_pair(f[k, r], edge[k], r)) for k in range(4)]
        totals, change = sums(pairs, both, eta, f[5, r])
        diagonal = both[0][0] + both[0][1] + inward + both[2][0] + both[2][1]
        for i, v in enumerate((*totals, change, diagonal, *both[0], *both[2])):
            parts_out[j, i] = v
    for j, r in enumerate((1, LAT - 2)):
        eta = f[4, r]
        inward = eta + f[4, 2 if r == 1 else r - 1]
        lat = lambda k: (None, s1[k, 2]) if r == 1 else (s1[k, r - 1], None)
        both = ((faces[0, r], faces[1, r]), (inward, inward), (faces[2, r], faces[3, r]))
        pairs = [(depth_pair(s1[k, r]), lat(k), lon_pair(s1[k, r], edge[6 + k], r)) for k in range(4)]
        totals, change = sums(pairs, both, eta, f[5, r])
        for i, v in enumerate((*totals, change, faces[4, r])):
            parts_out[2 + j, i] = v
        for k in range(4):
            s1_out[k, j] = s1[k, r]


def rim_kernel(f, edges, rows_first, rows_second, s1_in, parts, partial, whi, wlo, rim_out, values_out, lhs):
    is_above = first_above()
    south = lambda at: jnp.where(is_above, rows_second[at], rows_first[at])
    north = lambda at: jnp.where(is_above, rows_first[at], rows_second[at])
    low, high = south(CORNERS), north(CORNERS)

    group = iota(1) >> 2
    halo = [edges[k] for k in range(6)]
    totals, change, diagonal = [edges[12 + c] for c in range(3)], edges[15], edges[16]
    for upper, packed, row in ((False, low, 0), (True, high, LAT - 1)):
        lanes = 4 * row + 4
        corner = [jnp.where(group == row + 1, corner_columns(packed, k, not upper, lanes), 0.0) for k in range(5)]
        diagonal = diagonal + corner[4]
        totals, change = add_lat(totals, change, halo[4] + corner[4], halo[4], corner[:4], upper)
    edge1 = [swap_middle(v) for v in columns_done(halo, totals, change, diagonal)]
    low_edge, high_edge = swap_middle(low), swap_middle(high)

    def edge(k, r):
        if r < 0:
            return corner_columns(low_edge, k, True, LON - 2)
        if r >= LAT:
            return corner_columns(high_edge, k, False, LON - 2)
        return roll(edges[6 + k], 122 - 4 * r, 1)

    def field(k, r):
        if r < 0:
            return south(block(k if r == -2 else 5 + k))
        if r >= LAT:
            return north(block(k if r == LAT + 1 else 5 + k))
        return f[k, r]

    s1, new = {}, {}
    for j, r in enumerate((1, LAT - 2)):
        s1[r] = [s1_in[k, j] for k in range(4)]
    for j, (out, r, inward) in enumerate(((-1, 0, 1), (LAT, LAT - 1, LAT - 2))):
        upper = out > r
        order = (lambda a, b: (b, a)) if upper else (lambda a, b: (a, b))
        eta = field(4, out)
        far = 2 * out - r
        both, scale = faces_of(eta, (depth_pair(eta), order(field(4, far), field(4, r)), beside(eta, edge(4, out))))
        centre = [field(k, out) for k in range(4)]
        pairs = [(depth_pair(centre[k]), order(field(k, far), field(k, r)), beside(centre[k], edge(k, out))) for k in range(4)]
        s1[out] = [jnp.where(eta > 0.0, v, 0.0) for v in relax(centre, pairs, both, scale, eta, field(5, out))]
        eta = f[4, r]
        outward = eta + field(4, out)
        scale = OMEGA / (parts[j, 4] + outward)
        totals, change = add_lat([parts[j, c] for c in range(3)], parts[j, 3], outward, eta, [field(k, out) for k in range(4)], upper)
        s1[r] = settle([f[k, r] for k in range(4)], totals, change, scale)
        inner_face = eta + f[4, inward]
        both = ((parts[j, 5], parts[j, 6]), order(outward, inner_face), (parts[j, 7], parts[j, 8]))
        pairs = [(depth_pair(s1[r][k]), order(s1[out][k], s1[inward][k]), lon_pair(s1[r][k], edge1[k], r)) for k in range(4)]
        new[r] = relax(s1[r], pairs, both, scale, eta, f[5, r])
        totals, change = add_lat([parts[2 + j, c] for c in range(3)], parts[2 + j, 3], inner_face, f[4, inward], s1[r], upper)
        new[inward] = settle(s1[inward], totals, change, parts[2 + j, 4])
    for j, r in enumerate((0, 1, LAT - 2, LAT - 1)):
        t = f[5, r]
        new[r].append(advance(t, (depth_pair(t), (field(5, r - 1), field(5, r + 1)), beside(t, edge(5, r))), new[r]))
        for k in range(5):
            rim_out[k, j] = new[r][k]
            put_split(lhs, k, slice(j * LON, (j + 1) * LON), new[r][k])
    low, high = slice(0, 2 * LON), slice(14 * LON, 16 * LON)
    values_out[...] = (
        partial[...] + blend(lhs[:, : 2 * LON], whi[low], wlo[low]) + blend(lhs[:, 2 * LON :], whi[high], wlo[high])
    )


def place_kernel(mid, rim, values, table, struck, flow_out, warmth_out, lhs, out, sems):
    n = 5 * DEP
    v = values[...]
    top = v.astype(BF16)
    lhs[0:n] = top
    lhs[n : 2 * n] = (v - top.astype(F32)).astype(BF16)
    copies = []
    half = LAT // 2
    for g in range(2):
        placed = jnp.dot(lhs[...], table[:, g * half * LON : (g + 1) * half * LON], preferred_element_type=F32)
        merged = placed[:n] + placed[n : 2 * n]
        for h in range(half):
            r = g * half + h
            hit = struck[0:1, r * LON : (r + 1) * LON] > 0.5
            for k in range(5):
                kept = mid[k, r - 2] if 2 <= r < 14 else rim[k, r if r < 2 else r - 12]
                out[k, r] = jnp.where(hit, merged[k * DEP : (k + 1) * DEP, h * LON : (h + 1) * LON], kept)
        for r in range(g * half, (g + 1) * half):
            copies.append(pltpu.make_async_copy(out.at[0:4, r], flow_out.at[:, 0, :, r, :], sems.at[0, r]))
            copies.append(pltpu.make_async_copy(out.at[4, r], warmth_out.at[0, :, r, :], sems.at[1, r]))
            copies[-2].start()
            copies[-1].start()
    for c in copies:
        c.wait()


def shape(*dims, dtype=F32):
    return jax.ShapeDtypeStruct(dims, dtype)


def call(kernel, outs, ins, scratch=(), out_specs=None, flops=0, size=0, aliases=None, limit=None):
    return pl.pallas_call(
        kernel,
        out_shape=outs,
        in_specs=ins,
        out_specs=out_specs or [VMEM] * len(outs),
        scratch_shapes=list(scratch),
        input_output_aliases=aliases or {},
        cost_estimate=pl.CostEstimate(flops=flops, bytes_accessed=size, transcendentals=0),
        compiler_params=pltpu.CompilerParams(vmem_limit_bytes=limit or (32 << 20)),
    )


def in_hbm(x):
    return pltpu.with_memory_space_constraint(x, pltpu.HBM)


def shards(motion, warmth, label, chart, receivers, donors, factors):
    lon, lat = lax.axis_size("lon"), lax.axis_size("lat")
    n, slab = 5 * DEP, (DEP, LON)

    sides, rows = shape(DEP + DEP // 2, LON), shape(11 * DEP + 8, LON)
    f, cols, side_first, side_second, rows_first, rows_second, receivers, donors, factors = call(
        stage_kernel,
        [
            shape(6, LAT, *slab), shape(3, *slab), sides, sides, rows, rows,
            shape(1, 512, dtype=jnp.int32), shape(4, 512, dtype=jnp.int32), shape(4, 512),
        ],
        [HBM] * 7,
        [pltpu.VMEM((LAT,) + slab, jnp.int32), pltpu.SMEM((8,), F32), pltpu.SemaphoreType.DMA((4, LAT))],
        size=2 << 20,
    )(*map(in_hbm, (motion, warmth, label, chart, receivers.reshape(1, 512), donors.reshape(4, 512), factors.reshape(4, 512))))

    swap = lambda n, start: [(i + j, i + 1 - j) for i in range(start, n - 1, 2) for j in range(2)]
    cols_first = lax.ppermute(side_first, "lon", swap(lon, 1))
    cols_second = lax.ppermute(side_second, "lon", swap(lon, 0))
    whi, wlo = call(
        weights_kernel,
        [shape(LAT * LON, 512, dtype=BF16), shape(LAT * LON, 512, dtype=BF16)],
        [VMEM, VMEM],
        size=4 << 20,
        flops=20 << 20,
    )(donors, factors)
    rows_first, rows_second = call(
        corners_kernel,
        [rows, rows],
        [VMEM, VMEM, ANY, ANY, ANY],
        [pltpu.VMEM((8, LON), F32), pltpu.VMEM((8, LON), F32), pltpu.SemaphoreType.DMA((2,))],
        out_specs=[ANY, ANY],
        aliases={2: 0, 3: 1},
        size=1 << 16,
    )(cols_first, cols_second, rows_first, rows_second, whi)
    middle = middle_of(lon)
    outer = [b for b in range(lon) if b not in middle]
    among = lambda ones, start: [(b * lat + i, b * lat + j) for b in ones for i, j in swap(lat, start)]
    axes = ("lon", "lat")
    rows_in_first = lax.ppermute(rows_first, axes, among(middle, 1) + among(outer, 0))
    rows_in_second = lax.ppermute(rows_second, axes, among(middle, 0) + among(outer, 1))

    mid, partial, s1, edges, parts = call(
        inner_kernel,
        [shape(5, 12, *slab), shape(n, 512), shape(4, 2, *slab), shape(17, *slab), shape(4, 9, *slab)],
        [VMEM] * 6,
        [
            pltpu.VMEM((4, LAT) + slab, F32),
            pltpu.VMEM((5, LAT) + slab, F32),
            pltpu.VMEM((10,) + slab, F32),
            pltpu.VMEM((2 * n, 12 * LON), BF16),
        ],
        size=8 << 20,
        flops=1 << 30,
    )(f, cols, cols_first, cols_second, whi, wlo)
    rim, values = call(
        rim_kernel,
        [shape(5, 4, *slab), shape(n, 512)],
        [VMEM] * 9,
        [pltpu.VMEM((2 * n, 4 * LON), BF16)],
        size=2 << 20,
        flops=1 << 28,
    )(f, edges, rows_in_first, rows_in_second, s1, parts, partial, whi, wlo)

    mirror = [(p * lon + b, (1 - p) * lon + lon - 1 - b) for p in range(2) for b in range(lon)]
    incoming = lax.ppermute(values, ("panel", "lon"), mirror)

    table, struck = call(
        table_kernel,
        [shape(512, LAT * LON, dtype=BF16), shape(8, LAT * LON)],
        [VMEM],
        size=2 << 20,
        flops=4 << 20,
    )(receivers)

    flow, warm = call(
        place_kernel,
        [shape(4, 1, DEP, LAT, LON), shape(1, DEP, LAT, LON)],
        [VMEM] * 5,
        [pltpu.VMEM((2 * n, 512), BF16), pltpu.VMEM((5, LAT) + slab, F32), pltpu.SemaphoreType.DMA((2, LAT))],
        out_specs=[ANY, ANY],
        size=8 << 20,
        flops=1 << 30,
    )(mid, rim, incoming, table, struck)
    return flow, warm


def solution(mesh):
    field = P("panel", None, "lat", "lon")
    tile = ("panel", "lat", "lon")
    in_specs = (
        P(None, "panel", None, "lat", "lon"),
        field,
        field,
        P(),
        P(*tile, None),
        P(*tile, None, None),
        P(*tile, None, None),
    )
    out_specs = (P(None, "panel", None, "lat", "lon"), field)
    return jax.shard_map(shards, mesh=mesh, in_specs=in_specs, out_specs=out_specs, check_vma=False)
```
